256 devices in a mesh: section: 2 (over x_hi), cfg: 2 (over core), req: 4 (over y), sp: 16 (over x_lo, z).
Axes of the slice: x: 4 (x_hi: 2, x_lo: 2; x = x_hi * 2 + x_lo), y: 4, z: 8, core: 2. Of those that a mesh axis runs over, the one named last changes fastest.
Arguments:
- qkv: bfloat16 [2, 2, 10240, 3, 32, 128], P('section', 'cfg', ('req', 'sp')), parts along dimension 2, may hold values from -6 to 6
- counts: int32 [2, 4], P('section', 'req'), parts along dimension 1, may hold values from 1920 to 2560, as said below
- timesteps: int32 [2, 4], P('section', 'req'), parts along dimension 1, may hold values from 0 to 999
- block_map: int32 [10240], P(('req', 'sp')), parts along dimension 0, may hold values from 0 to 2559
- w_out: bfloat16 [32, 128, 64], replicated, may hold values from -0.09375 to 0.09375
- w_in: bfloat16 [64, 32, 128], replicated, may hold values from -0.75 to 0.75
Outputs:
- result: bfloat16 [2, 10240, 2, 16, 128], P('section', ('req', 'sp'), 'cfg'), parts along dimension 1
The draws below stay inside these ranges and needn't reach their ends.
There are 4 independent parts, one for each index of `req`. The reference program is written for one: setup_inputs(seed, part) draws one part's arguments, and reference() takes and returns one part's arrays. A program takes and returns all parts, laid end to end along the dimension named above; an argument that names none is the same for every part. Nothing has to cross between parts.
Inputs may be any that keep to these rules, and one draw needn't show every extreme that they name: `counts`: at least 1920 in both sections, and exactly 2560 in one of them.
All inputs are finite; a program needn't handle non-finite values.
Results may differ from the reference program's by a relative error of at most 0.008.
Values may be sent and summed in bfloat16 or wider, within the bound.
A program may use at most 64 MiB of HBM per device.

```python
import math
import jax
import jax.numpy as jnp
from jax import lax

HEADS = 32
HD = 128
LATENT = 64
TOKENS = 2560


def draw_qkv(key, part):
    key = jax.random.fold_in(key, 11)
    key_vals = jax.random.fold_in(key, 0)
    shape = (2, 2, TOKENS, 3, HEADS, HD)
    slot_scale = jnp.array([1.4, 1.4, 1.0], jnp.float32).reshape(1, 1, 1, 3, 1, 1)
    values = jnp.clip(jax.random.normal(key_vals, shape, jnp.float32) * slot_scale, -6.0, 6.0)
    return values.astype(jnp.bfloat16)


def draw_counts(key, part):
    key = jax.random.fold_in(key, 23)
    key_pick, key_short = jax.random.split(key)
    pick = jax.random.randint(key_pick, (), 0, 2)
    short = jax.random.randint(key_short, (2, 1), 3 * TOKENS // 4, TOKENS)
    rows = jnp.arange(2).reshape(2, 1)
    return jnp.where(rows == pick, TOKENS, short).astype(jnp.int32)


def place_ends(entries, stream_key, low, high):
    longest = entries.shape.index(max(entries.shape))
    spots = []
    for shift in (0, 1):
        where = [jax.random.randint(jax.random.fold_in(stream_key, axis), (), 0, length) for axis, length in enumerate(entries.shape)]
        where[longest] = (where[longest] + shift) % entries.shape[longest]
        spots.append(tuple(where))
    return entries.at[spots[0]].set(low).at[spots[1]].set(high)


def gaussian(own_key, shape, spread, reach, dtype=jnp.bfloat16):
    values = spread * jax.random.normal(own_key, shape, jnp.float32)
    return jnp.clip(values, min=-reach, max=reach).astype(dtype)


def setup_inputs(seed: int = 0, part: int = 0) -> dict:
    splits = jax.random.split(jax.random.key(seed), 7)
    part_splits = jax.random.split(jax.random.fold_in(splits[6], part), 7)
    return {
        "qkv": draw_qkv(jax.random.fold_in(jax.random.fold_in(splits[6], part), 71), part),
        "counts": draw_counts(jax.random.fold_in(jax.random.fold_in(splits[6], part), 71), part),
        "timesteps": jax.random.randint(part_splits[2], (2, 1), 0, 1000).astype(jnp.int32),
        "block_map": place_ends(jax.random.randint(part_splits[3], (TOKENS,), 0, TOKENS), jax.random.fold_in(part_splits[3], 1), 0, TOKENS - 1).astype(jnp.int32),
        "w_out": gaussian(splits[4], (HEADS, HD, LATENT), (HEADS * HD) ** -0.5, 0.09375),
        "w_in": gaussian(splits[5], (LATENT, HEADS, HD), LATENT ** -0.5, 0.75),
    }


def attend_head(parts, count):
    query, keys, values = parts[0], parts[1], parts[2]
    scores = jnp.dot(query, keys.T, preferred_element_type=jnp.float32) * (HD ** -0.5)
    keys_ok = (jnp.arange(TOKENS) < count)[None, :]
    scores = jnp.where(keys_ok, scores, -1e30)
    top = jnp.max(scores, axis=-1, keepdims=True)
    expo = jnp.where(keys_ok, jnp.exp(scores - top), 0.0)
    total = jnp.sum(expo, axis=-1, keepdims=True)
    mixed = jnp.dot(expo.astype(jnp.bfloat16), values, preferred_element_type=jnp.float32) / total
    return mixed.astype(jnp.bfloat16)


def branch_out(block, count):
    ordered = jnp.transpose(block, (2, 1, 0, 3))
    heads_out = lax.map(lambda parts: attend_head(parts, count), ordered)
    return jnp.transpose(heads_out, (1, 0, 2))


def gate_table(tstep):
    head_ids = jnp.arange(HEADS).astype(jnp.float32)
    dims = jnp.arange(HD).astype(jnp.float32)
    freq = jnp.exp(-math.log(10000.0) * dims / HD)
    return 1.0 + 0.5 * jnp.sin(tstep.astype(jnp.float32) * freq[None, :] + 0.7 * head_ids[:, None])


def reference(qkv, counts, timesteps, block_map, w_out, w_in):
    branches = []
    for section in range(2):
        count = counts[section, 0]
        cond = branch_out(qkv[section, 0], count).astype(jnp.float32)
        uncond = branch_out(qkv[section, 1], count).astype(jnp.float32)
        guided = uncond + 5.0 * (cond - uncond)
        valid = (jnp.arange(TOKENS) < count).astype(jnp.float32)
        gate = gate_table(timesteps[section, 0])
        branches.append((gate[None] * guided * valid[:, None, None]).astype(jnp.bfloat16))
    latent = jnp.einsum("thd,hdl->tl", branches[0].astype(jnp.float32), w_out.astype(jnp.float32)).astype(jnp.bfloat16)
    picked = jnp.take(latent, block_map, axis=0)
    lifted = jnp.einsum("tl,lhd->thd", picked.astype(jnp.float32), w_in.astype(jnp.float32))
    upper = (branches[1].astype(jnp.float32) + lifted).astype(jnp.bfloat16)
    stacked = jnp.stack([branches[0], upper], axis=0)
    stacked = stacked.reshape(2, TOKENS, HEADS // 2, 2, HD)
    return jnp.transpose(stacked, (0, 1, 3, 2, 4))
```

```python
import math

import jax
import jax.numpy as jnp
from jax import lax
from jax.experimental import pallas as pl
from jax.experimental.pallas import tpu as pltpu
from jax.sharding import PartitionSpec as P

MESH = pl.DeviceIdType.MESH
F32 = jnp.float32
BF16 = jnp.bfloat16


def kernel(
    n_sp, tok, heads, hd, width,
    qkv_ref, cnt_ref, ts_ref, bm_ref, wo_ref, wi_ref, out_ref,
    xin, stage, qland, kland, vaug, kt, sc, att_mine, att_send, att_recv, brs, brl,
    lat_mine, lat_recv, psum_send, psum_recv, onehot, wo, wi, w2, gate,
    in_sem, w_sem, own_sem, s_sem, r_sem, sib_s, sib_r, br_s, br_r, ps_s, ps_r, lat_s, lat_r,
):
    seq = tok * n_sp
    half = tok // 2
    n_z = n_sp // 2
    sec = lax.axis_index("section")
    core = lax.axis_index("cfg")
    me = lax.axis_index("sp")
    count = cnt_ref[0, 0]
    scale = hd ** -0.5 * math.log2(math.e)

    def offset(step):
        turn = step // 2
        dz = ((turn + 1) // 2) * (1 - 2 * ((turn + 1) % 2))
        return step % 2, dz

    def to_peer(step):
        dx, dz = offset(step)
        return ((me // n_z + dx) % 2) * n_z + (me % n_z + dz + n_z) % n_z

    def from_peer(step):
        dx, dz = offset(step)
        return ((me // n_z + dx) % 2) * n_z + (me % n_z - dz + n_z) % n_z

    loads = [
        pltpu.make_async_copy(qkv_ref.at[:, c], xin.at[c], in_sem.at[c]) for c in (0, 1, 2)
    ]
    for c in (1, 2, 0):
        loads[c].start()
    load_wo = pltpu.make_async_copy(wo_ref, wo, w_sem.at[0])
    load_wi = pltpu.make_async_copy(wi_ref, wi, w_sem.at[1])
    load_wo.start()
    load_wi.start()

    barrier = pltpu.get_barrier_semaphore()

    def greet(step, carry):
        peer = to_peer(step)
        pl.semaphore_signal(barrier, inc=1, device_id={"sp": peer}, device_id_type=MESH)
        pl.semaphore_signal(
            barrier, inc=1, device_id={"section": 1 - sec, "sp": peer}, device_id_type=MESH
        )
        return carry

    lax.fori_loop(1, n_sp, greet, 0)
    pl.semaphore_signal(barrier, inc=1, device_id={"cfg": 1 - core}, device_id_type=MESH)
    pl.semaphore_signal(barrier, inc=1, device_id={"section": 1 - sec}, device_id_type=MESH)

    def transpose_kind(c):
        def body(t, carry):
            rows = pl.ds(pl.multiple_of(t * 16, 16), 16)
            stage[c, :, rows, :] = jnp.swapaxes(xin[c, rows], 0, 1)
            return carry

        lax.fori_loop(0, tok // 16, body, 0)

    def landing(c, source):
        if c == 0:
            return qland.at[source]
        rows = pl.ds(pl.multiple_of(source * tok, tok), tok)
        if c == 1:
            return kland.at[:, rows, :]
        return vaug.at[:, rows, pl.ds(0, hd)]

    def qkv_copy(c, target):
        return pltpu.make_async_remote_copy(
            src_ref=stage.at[c, pl.ds(2 * target, 2)],
            dst_ref=landing(c, me),
            send_sem=s_sem.at[c, target],
            recv_sem=r_sem.at[c, me],
            device_id={"sp": target},
            device_id_type=MESH,
        )

    def qkv_arrival(c, source):
        return pltpu.make_async_remote_copy(
            src_ref=stage.at[c, pl.ds(2 * source, 2)],
            dst_ref=landing(c, source),
            send_sem=s_sem.at[c, source],
            recv_sem=r_sem.at[c, source],
            device_id={"sp": source},
            device_id_type=MESH,
        )

    def own_copy(c):
        return pltpu.make_async_copy(
            stage.at[c, pl.ds(2 * me, 2)], landing(c, me), own_sem.at[c]
        )

    def send_kind(c):
        def body(step, carry):
            qkv_copy(c, to_peer(step)).start()
            return carry

        lax.fori_loop(1, n_sp, body, 0)
        own_copy(c).start()

    loads[1].wait()
    transpose_kind(1)
    pl.semaphore_wait(barrier, 2 * n_sp)
    send_kind(1)
    loads[2].wait()
    transpose_kind(2)
    send_kind(2)
    loads[0].wait()
    transpose_kind(0)
    send_kind(0)

    head_id = (2 * me + core).astype(F32)
    dims = lax.broadcasted_iota(jnp.int32, (8, hd), 1).astype(F32)
    freq = jnp.exp(-math.log(10000.0) * dims / hd)
    gate[...] = 1.0 + 0.5 * jnp.sin(ts_ref[0, 0].astype(F32) * freq + 0.7 * head_id)

    key_rows = lax.broadcasted_iota(jnp.int32, (seq, hd), 0)
    ones = jnp.where(key_rows < count, 1.0, 0.0).astype(BF16)
    vaug[0, :, hd:] = ones
    vaug[1, :, hd:] = ones

    load_wo.wait()
    load_wi.wait()

    @pl.when(sec == 1)
    def _():
        def turn(t, carry):
            rows = pl.ds(pl.multiple_of(t * 16, 16), 16)
            stacked = jnp.swapaxes(wi[rows], 0, 1).reshape(heads // 2, 2, 16, hd)
            part = jnp.where(core == 0, stacked[:, 0], stacked[:, 1])
            w2[:, rows, :] = part
            w2[:, pl.ds(pl.multiple_of(width + t * 16, 16), 16), :] = part
            return carry

        lax.fori_loop(0, width // 16, turn, 0)
        eye = lax.broadcasted_iota(jnp.int32, (tok, tok), 0) == lax.broadcasted_iota(
            jnp.int32, (tok, tok), 1
        )
        wanted = jnp.sum(
            jnp.where(eye, jnp.broadcast_to(bm_ref[...], (tok, tok)).astype(F32), 0.0),
            axis=1, keepdims=True,
        ).astype(jnp.int32)
        owner = wanted // tok
        row = wanted - owner * tok
        upper = (row >= half).astype(jnp.int32)
        slot = owner * half + row - upper * half
        places = lax.broadcasted_iota(jnp.int32, (tok, n_sp * half), 1)
        onehot[0] = jnp.where(places == jnp.where(upper == 0, slot, -1), 1.0, 0.0).astype(BF16)
        onehot[1] = jnp.where(places == jnp.where(upper == 1, slot, -1), 1.0, 0.0).astype(BF16)

    def wait_kind(c):
        def body(step, carry):
            qkv_arrival(c, from_peer(step)).wait_recv()
            return carry

        lax.fori_loop(1, n_sp, body, 0)
        own_copy(c).wait()

    quarter = seq // 4
    tail_ok = 3 * quarter + lax.broadcasted_iota(jnp.int32, (quarter, hd), 0) < count
    wait_kind(1)
    for h in (0, 1):
        for part in range(4):
            rows = slice(part * quarter, (part + 1) * quarter)
            block = kland[h, rows].astype(F32)
            if part == 3:
                block = jnp.where(tail_ok, block, kland[h, 0:16].astype(F32)[0:1])
            kt[h, :, rows] = block.T.astype(BF16)
    wait_kind(2)
    for h in (0, 1):
        tail = vaug[h, 3 * quarter:, :hd].astype(F32)
        vaug[h, 3 * quarter:, :hd] = jnp.where(tail_ok, tail, 0.0).astype(BF16)

    def sibling_copy(source):
        return pltpu.make_async_remote_copy(
            src_ref=att_send.at[source],
            dst_ref=att_recv.at[source],
            send_sem=sib_s.at[source],
            recv_sem=sib_r.at[source],
            device_id={"cfg": 1 - core},
            device_id_type=MESH,
        )

    def branch_copy(target):
        return pltpu.make_async_remote_copy(
            src_ref=brs.at[target],
            dst_ref=brl.at[me],
            send_sem=br_s.at[target],
            recv_sem=br_r.at[me],
            device_id={"sp": target},
            device_id_type=MESH,
        )

    def branch_arrival(source):
        return pltpu.make_async_remote_copy(
            src_ref=brs.at[source],
            dst_ref=brl.at[source],
            send_sem=br_s.at[source],
            recv_sem=br_r.at[source],
            device_id={"sp": source},
            device_id_type=MESH,
        )

    def attend(step):
        source = from_peer(step)
        for h in (0, 1):
            sc[h] = jnp.dot(qland[source, h], kt[h], preferred_element_type=F32)
        done = []
        for h in (0, 1):
            top = jnp.max(sc[h], axis=1, keepdims=True) * scale
            weights = jnp.exp2(sc[h] * scale - top).astype(BF16)
            mixed = jnp.dot(weights, vaug[h], preferred_element_type=F32)
            done.append(mixed[:, :hd] / mixed[:, hd:])
        att_mine[source] = jnp.where(core == 0, done[0], done[1]).astype(BF16)
        att_send[source] = jnp.where(core == 0, done[1], done[0]).astype(BF16)
        sibling_copy(source).start()

    def combine(step):
        source = from_peer(step)
        sibling_copy(source).wait_recv()
        mine = att_mine[source].astype(F32)
        theirs = att_recv[source].astype(F32)
        cond = jnp.where(core == 0, mine, theirs)
        uncond = jnp.where(core == 0, theirs, mine)
        guided = uncond + 5.0 * (cond - uncond)
        position = source * tok + lax.broadcasted_iota(jnp.int32, (tok, hd), 0)
        return source, jnp.where(position < count, gate[0:1] * guided, 0.0).astype(BF16)

    def send_branch(step):
        target, block = combine(step)
        brs[target] = block
        branch_copy(target).start()

    own_copy(0).wait()
    attend(0)

    def first(step, carry):
        qkv_arrival(0, from_peer(step)).wait_recv()
        attend(step)

        @pl.when(step == 1)
        def _():
            source, block = combine(0)
            brl[source] = block

        @pl.when(step > 1)
        def _():
            send_branch(step - 1)

        return carry

    lax.fori_loop(1, n_sp, first, 0)
    send_branch(n_sp - 1)

    @pl.when(sec == 0)
    def _():
        def project(step, total):
            source = from_peer(step)

            @pl.when(step > 0)
            def _():
                branch_arrival(source).wait_recv()

            block = brl[source]
            out_ref[source] = block
            return total + lax.dot_general(
                block, wo[2 * source + core], (((1,), (1,)), ((), ())),
                preferred_element_type=F32,
            )

        total = lax.fori_loop(0, n_sp, project, jnp.zeros((tok, width), F32))
        packed = jnp.concatenate([total[:half], total[half:]], axis=1)
        psum_send[...] = packed
        swap = pltpu.make_async_remote_copy(
            src_ref=psum_send, dst_ref=psum_recv, send_sem=ps_s, recv_sem=ps_r,
            device_id={"cfg": 1 - core}, device_id_type=MESH,
        )
        swap.start()
        swap.wait_recv()
        lat_mine[...] = (packed + psum_recv[...]).astype(BF16)

        def hand(step, carry):
            target = to_peer(step)
            pltpu.make_async_remote_copy(
                src_ref=lat_mine, dst_ref=lat_recv.at[me], send_sem=lat_s.at[target],
                recv_sem=lat_r.at[me], device_id={"section": 1, "sp": target},
                device_id_type=MESH,
            ).start()
            return carry

        lax.fori_loop(0, n_sp, hand, 0)

        def handed(step, carry):
            target = to_peer(step)
            pltpu.make_async_remote_copy(
                src_ref=lat_mine, dst_ref=lat_recv.at[me], send_sem=lat_s.at[target],
                recv_sem=lat_r.at[me], device_id={"section": 1, "sp": target},
                device_id_type=MESH,
            ).wait_send()
            return carry

        lax.fori_loop(0, n_sp, handed, 0)
        swap.wait_send()

    @pl.when(sec == 1)
    def _():
        def arrived(step, carry):
            branch_arrival(from_peer(step)).wait_recv()
            return carry

        lax.fori_loop(1, n_sp, arrived, 0)

        def latent_in(step, carry):
            source = from_peer(step)
            pltpu.make_async_remote_copy(
                src_ref=lat_mine, dst_ref=lat_recv.at[source], send_sem=lat_s.at[source],
                recv_sem=lat_r.at[source], device_id={"section": 0, "sp": source},
                device_id_type=MESH,
            ).wait_recv()
            return carry

        lax.fori_loop(0, n_sp, latent_in, 0)
        table = lat_recv[...].reshape(n_sp * half, 2 * width)
        low = jnp.dot(onehot[0], table, preferred_element_type=F32)
        high = jnp.dot(onehot[1], table, preferred_element_type=F32)
        lanes = lax.broadcasted_iota(jnp.int32, (tok, 2 * width), 1)
        picked = jnp.where(lanes < width, low, high).astype(BF16)

        def lift(g, carry):
            lifted = jnp.dot(picked, w2[g], preferred_element_type=F32)
            out_ref[g] = (brl[g].astype(F32) + lifted).astype(BF16)
            return carry

        lax.fori_loop(0, n_sp, lift, 0)

    def drain(step, carry):
        target = to_peer(step)
        for c in (0, 1, 2):
            qkv_copy(c, target).wait_send()
        branch_copy(target).wait_send()
        sibling_copy(target).wait_send()
        return carry

    lax.fori_loop(1, n_sp, drain, 0)
    sibling_copy(me).wait_send()


def on_device(qkv, counts, timesteps, block_map, w_out, w_in):
    n_sp = lax.axis_size("sp")
    tok, _, heads, hd = qkv.shape[2:]
    width = w_out.shape[2]
    seq = tok * n_sp
    half = tok // 2
    dma = pltpu.SemaphoreType.DMA
    smem = pl.BlockSpec(memory_space=pltpu.SMEM)
    vmem = pl.BlockSpec(memory_space=pltpu.VMEM)
    hbm = pl.BlockSpec(memory_space=pl.ANY)

    def body(*refs):
        kernel(n_sp, tok, heads, hd, width, *refs)

    by_head = pl.pallas_call(
        body,
        name="guided_attention",
        out_shape=jax.ShapeDtypeStruct((heads // 2, tok, hd), BF16),
        in_specs=[hbm, smem, smem, vmem, hbm, hbm],
        out_specs=vmem,
        scratch_shapes=[
            pltpu.VMEM((3, tok, heads, hd), BF16),
            pltpu.VMEM((3, heads, tok, hd), BF16),
            pltpu.VMEM((n_sp, 2, tok, hd), BF16),
            pltpu.VMEM((2, seq, hd), BF16),
            pltpu.VMEM((2, seq, 2 * hd), BF16),
            pltpu.VMEM((2, hd, seq), BF16),
            pltpu.VMEM((2, tok, seq), F32),
            pltpu.VMEM((n_sp, tok, hd), BF16),
            pltpu.VMEM((n_sp, tok, hd), BF16),
            pltpu.VMEM((n_sp, tok, hd), BF16),
            pltpu.VMEM((n_sp, tok, hd), BF16),
            pltpu.VMEM((n_sp, tok, hd), BF16),
            pltpu.VMEM((half, 2 * width), BF16),
            pltpu.VMEM((n_sp, half, 2 * width), BF16),
            pltpu.VMEM((half, 2 * width), F32),
            pltpu.VMEM((half, 2 * width), F32),
            pltpu.VMEM((2, tok, n_sp * half), BF16),
            pltpu.VMEM((heads, width, hd), BF16),
            pltpu.VMEM((width, heads, hd), BF16),
            pltpu.VMEM((heads // 2, 2 * width, hd), BF16),
            pltpu.VMEM((8, hd), F32),
            dma((3,)), dma((2,)), dma((3,)),
            dma((3, n_sp)), dma((3, n_sp)),
            dma((n_sp,)), dma((n_sp,)),
            dma((n_sp,)), dma((n_sp,)),
            dma, dma,
            dma((n_sp,)), dma((n_sp,)),
        ],
        compiler_params=pltpu.CompilerParams(
            collective_id=0, has_side_effects=True, vmem_limit_bytes=56 << 20
        ),
    )(
        qkv[0, 0],
        counts,
        timesteps,
        block_map.reshape(1, tok),
        jnp.swapaxes(w_out, 1, 2),
        w_in,
    )
    return jnp.swapaxes(by_head, 0, 1)[None, :, None]


def solution(mesh):
    placed = (
        P("section", "cfg", ("req", "sp"), None, None, None),
        P("section", "req"),
        P("section", "req"),
        P(("req", "sp")),
        P(),
        P(),
    )
    return jax.shard_map(
        on_device,
        mesh=mesh,
        in_specs=placed,
        out_specs=P("section", ("req", "sp"), "cfg", None, None),
        check_vma=False,
    )
```

```python
import math

import jax
import jax.numpy as jnp
from jax import lax
from jax.experimental import pallas as pl
from jax.experimental.pallas import tpu as pltpu
from jax.sharding import PartitionSpec as P

MESH = pl.DeviceIdType.MESH
F32 = jnp.float32
BF16 = jnp.bfloat16
HOLD = 8


def kernel(
    n_sp, tok, heads, hd, width,
    qkv_ref, cnt_ref, ts_ref, bm_ref, wo_ref, wi_ref, out_ref,
    xin, stage, qland, kland, vaug, kt, sc, att_mine, att_send, att_recv, brs, brl,
    lat_mine, lat_a, lat_b, psum_send, psum_recv, onehot_a, onehot_b, wo, wi, w2, gate, lifted,
    cnt, ts, bm,
    in_sem, w_sem, own_sem, s_sem, r_sem, sib_s, sib_r, br_s, br_r, ps_s, ps_r, lat_s, lat_r,
):
    seq = tok * n_sp
    part_a = tok // 32 // 2 * 32 + tok // 32 % 2 * 32
    parts = ((0, part_a), (part_a, tok - part_a))
    n_z = n_sp // 2
    sec = lax.axis_index("section")
    core = lax.axis_index("cfg")
    me = lax.axis_index("sp")
    scale = hd ** -0.5 * math.log2(math.e)

    def offset(step):
        turn = step // 2
        dz = ((turn + 1) // 2) * (1 - 2 * ((turn + 1) % 2))
        return step % 2, dz

    def to_peer(step):
        dx, dz = offset(step)
        return ((me // n_z + dx) % 2) * n_z + (me % n_z + dz + n_z) % n_z

    def from_peer(step):
        dx, dz = offset(step)
        return ((me // n_z + dx) % 2) * n_z + (me % n_z - dz + n_z) % n_z

    loads = [
        pltpu.make_async_copy(qkv_ref.at[:, c], xin.at[c], in_sem.at[c]) for c in (0, 1, 2)
    ]
    loads[1].start()
    smalls = [
        pltpu.make_async_copy(source, held, w_sem.at[n])
        for n, (source, held) in enumerate(
            ((wo_ref, wo), (wi_ref, wi), (cnt_ref, cnt), (ts_ref, ts), (bm_ref, bm))
        )
    ]

    barrier = pltpu.get_barrier_semaphore()

    def greet(step, carry):
        peer = to_peer(step)
        pl.semaphore_signal(barrier, inc=1, device_id={"sp": peer}, device_id_type=MESH)
        return carry

    lax.fori_loop(1, n_sp, greet, 0)
    pl.semaphore_signal(barrier, inc=1, device_id={"cfg": 1 - core}, device_id_type=MESH)
    pl.semaphore_signal(barrier, inc=1, device_id={"section": 1 - sec}, device_id_type=MESH)

    def transpose_kind(c):
        def body(t, carry):
            rows = pl.ds(pl.multiple_of(t * 16, 16), 16)
            stage[c, :, rows, :] = jnp.swapaxes(xin[c, rows], 0, 1)
            return carry

        lax.fori_loop(0, tok // 16, body, 0)

    def landing(c, source):
        if c == 0:
            return qland.at[source]
        rows = pl.ds(pl.multiple_of(source * tok, tok), tok)
        if c == 1:
            return kland.at[:, rows, :]
        return vaug.at[:, rows, pl.ds(0, hd)]

    def qkv_copy(c, target):
        return pltpu.make_async_remote_copy(
            src_ref=stage.at[c, pl.ds(2 * target, 2)],
            dst_ref=landing(c, me),
            send_sem=s_sem.at[c, target],
            recv_sem=r_sem.at[c, me],
            device_id={"sp": target},
            device_id_type=MESH,
        )

    def qkv_arrival(c, source):
        return pltpu.make_async_remote_copy(
            src_ref=stage.at[c, pl.ds(2 * source, 2)],
            dst_ref=landing(c, source),
            send_sem=s_sem.at[c, source],
            recv_sem=r_sem.at[c, source],
            device_id={"sp": source},
            device_id_type=MESH,
        )

    def own_copy(c):
        return pltpu.make_async_copy(
            stage.at[c, pl.ds(2 * me, 2)], landing(c, me), own_sem.at[c]
        )

    def send_kind(c):
        def body(step, carry):
            qkv_copy(c, to_peer(step)).start()
            return carry

        lax.fori_loop(1, n_sp, body, 0)
        own_copy(c).start()

    loads[1].wait()
    loads[2].start()
    loads[0].start()
    for small in smalls:
        small.start()
    transpose_kind(1)
    pl.semaphore_wait(barrier, n_sp + 1)
    send_kind(1)
    loads[2].wait()
    transpose_kind(2)
    send_kind(2)
    loads[0].wait()
    transpose_kind(0)
    send_kind(0)

    for small in smalls:
        small.wait()
    count = cnt[0, 0]
    head_id = (2 * me + core).astype(F32)
    dims = lax.broadcasted_iota(jnp.int32, (8, hd), 1).astype(F32)
    freq = jnp.exp(-math.log(10000.0) * dims / hd)
    gate[...] = 1.0 + 0.5 * jnp.sin(ts[0, 0].astype(F32) * freq + 0.7 * head_id)

    key_rows = lax.broadcasted_iota(jnp.int32, (seq, hd), 0)
    ones = jnp.where(key_rows < count, 1.0, 0.0).astype(BF16)
    vaug[0, :, hd:] = ones
    vaug[1, :, hd:] = ones

    @pl.when(sec == 1)
    def _():
        def turn(t, carry):
            rows = pl.ds(pl.multiple_of(t * 16, 16), 16)
            stacked = jnp.swapaxes(wi[rows], 0, 1).reshape(heads // 2, 2, 16, hd)
            part = jnp.where(core == 0, stacked[:, 0], stacked[:, 1])
            w2[:, rows, :] = part
            w2[:, pl.ds(pl.multiple_of(width + t * 16, 16), 16), :] = part
            return carry

        lax.fori_loop(0, width // 16, turn, 0)
        eye = lax.broadcasted_iota(jnp.int32, (tok, tok), 0) == lax.broadcasted_iota(
            jnp.int32, (tok, tok), 1
        )
        wanted = jnp.sum(
            jnp.where(eye, jnp.broadcast_to(bm[...], (tok, tok)).astype(F32), 0.0),
            axis=1, keepdims=True,
        ).astype(jnp.int32)
        owner = wanted // tok
        row = wanted - owner * tok
        for onehot, (start, size) in ((onehot_a, parts[0]), (onehot_b, parts[1])):
            depth = size // 2
            inside = row - start
            upper = (inside >= depth).astype(jnp.int32)
            slot = owner * depth + inside - upper * depth
            here = jnp.logical_and(inside >= 0, inside < size)
            places = lax.broadcasted_iota(jnp.int32, (tok, n_sp * depth), 1)
            for side in (0, 1):
                target = jnp.where(jnp.logical_and(here, upper == side), slot, -1)
                onehot[side] = jnp.where(places == target, 1.0, 0.0).astype(BF16)

    def wait_kind(c):
        def body(step, carry):
            qkv_arrival(c, from_peer(step)).wait_recv()
            return carry

        lax.fori_loop(1, n_sp, body, 0)
        own_copy(c).wait()

    quarter = seq // 4
    tail_ok = 3 * quarter + lax.broadcasted_iota(jnp.int32, (quarter, hd), 0) < count
    wait_kind(1)
    for h in (0, 1):
        for part in range(4):
            rows = slice(part * quarter, (part + 1) * quarter)
            block = kland[h, rows].astype(F32)
            if part == 3:
                block = jnp.where(tail_ok, block, kland[h, 0:16].astype(F32)[0:1])
            kt[h, :, rows] = block.T.astype(BF16)
    wait_kind(2)
    for h in (0, 1):
        tail = vaug[h, 3 * quarter:, :hd].astype(F32)
        vaug[h, 3 * quarter:, :hd] = jnp.where(tail_ok, tail, 0.0).astype(BF16)

    def sibling_copy(source):
        return pltpu.make_async_remote_copy(
            src_ref=att_send.at[source],
            dst_ref=att_recv.at[source],
            send_sem=sib_s.at[source],
            recv_sem=sib_r.at[source],
            device_id={"cfg": 1 - core},
            device_id_type=MESH,
        )

    def branch_copy(part, target):
        rows = pl.ds(*parts[part])
        return pltpu.make_async_remote_copy(
            src_ref=brs.at[target, rows],
            dst_ref=brl.at[me, rows],
            send_sem=br_s.at[part, target],
            recv_sem=br_r.at[part, me],
            device_id={"sp": target},
            device_id_type=MESH,
        )

    def branch_arrival(part, source):
        rows = pl.ds(*parts[part])
        return pltpu.make_async_remote_copy(
            src_ref=brs.at[source, rows],
            dst_ref=brl.at[source, rows],
            send_sem=br_s.at[part, source],
            recv_sem=br_r.at[part, source],
            device_id={"sp": source},
            device_id_type=MESH,
        )

    def attend(step):
        source = from_peer(step)
        for h in (0, 1):
            sc[h] = jnp.dot(qland[source, h], kt[h], preferred_element_type=F32)
        done = []
        for h in (0, 1):
            top = jnp.max(sc[h], axis=1, keepdims=True) * scale
            weights = jnp.exp2(sc[h] * scale - top).astype(BF16)
            mixed = jnp.dot(weights, vaug[h], preferred_element_type=F32)
            done.append(mixed[:, :hd] / mixed[:, hd:])
        att_mine[source] = jnp.where(core == 0, done[0], done[1]).astype(BF16)
        att_send[source] = jnp.where(core == 0, done[1], done[0]).astype(BF16)
        sibling_copy(source).start()

    def combine(step):
        source = from_peer(step)
        sibling_copy(source).wait_recv()
        mine = att_mine[source].astype(F32)
        theirs = att_recv[source].astype(F32)
        cond = jnp.where(core == 0, mine, theirs)
        uncond = jnp.where(core == 0, theirs, mine)
        guided = uncond + 5.0 * (cond - uncond)
        position = source * tok + lax.broadcasted_iota(jnp.int32, (tok, hd), 0)
        return source, jnp.where(position < count, gate[0:1] * guided, 0.0).astype(BF16)

    def keep(step):
        target, block = combine(step)
        brs[target] = block

    def send_part(part, step):
        branch_copy(part, from_peer(step)).start()

    own_copy(0).wait()
    attend(0)

    def first(step, carry):
        qkv_arrival(0, from_peer(step)).wait_recv()
        attend(step)

        @pl.when(step == 1)
        def _():
            source, block = combine(0)
            brl[source] = block

        @pl.when(step > 1)
        def _():
            keep(step - 1)

        return carry

    def release(step, carry):
        send_part(0, step)
        return carry

    def later(step, carry):
        qkv_arrival(0, from_peer(step)).wait_recv()
        attend(step)
        keep(step - 1)
        send_part(0, step - 1)
        return carry

    hold = n_sp - 1 if n_sp < HOLD else HOLD
    lax.fori_loop(1, hold, first, 0)
    lax.fori_loop(1, hold - 1, release, 0)
    lax.fori_loop(hold, n_sp, later, 0)
    keep(n_sp - 1)
    send_part(0, n_sp - 1)

    def second(step, carry):
        send_part(1, step)
        return carry

    lax.fori_loop(1, n_sp, second, 0)

    def swap_copy(part):
        rows = pl.ds(parts[part][0] // 2, parts[part][1] // 2)
        return pltpu.make_async_remote_copy(
            src_ref=psum_send.at[rows], dst_ref=psum_recv.at[rows],
            send_sem=ps_s.at[part], recv_sem=ps_r.at[part],
            device_id={"cfg": 1 - core}, device_id_type=MESH,
        )

    def latent_copy(part, target):
        rows = pl.ds(parts[part][0] // 2, parts[part][1] // 2)
        return pltpu.make_async_remote_copy(
            src_ref=lat_mine.at[rows], dst_ref=(lat_a, lat_b)[part].at[me],
            send_sem=lat_s.at[part, target], recv_sem=lat_r.at[part, me],
            device_id={"section": 1, "sp": target}, device_id_type=MESH,
        )

    def latent_arrival(part, source):
        rows = pl.ds(parts[part][0] // 2, parts[part][1] // 2)
        return pltpu.make_async_remote_copy(
            src_ref=lat_mine.at[rows], dst_ref=(lat_a, lat_b)[part].at[source],
            send_sem=lat_s.at[part, source], recv_sem=lat_r.at[part, source],
            device_id={"section": 0, "sp": source}, device_id_type=MESH,
        )

    def turn_out(blocks):
        def body(t, carry):
            rows = pl.ds(pl.multiple_of(t * 16, 16), 16)
            out_ref[rows] = jnp.swapaxes(blocks[:, rows, :], 0, 1)
            return carry

        lax.fori_loop(0, tok // 16, body, 0)

    @pl.when(sec == 0)
    def _():
        for part, (start, size) in enumerate(parts):
            def project(step, total, part=part, start=start, size=size):
                source = from_peer(step)

                @pl.when(step > 0)
                def _():
                    branch_arrival(part, source).wait_recv()

                return total + lax.dot_general(
                    brl[source, start:start + size], wo[2 * source + core],
                    (((1,), (1,)), ((), ())), preferred_element_type=F32,
                )

            total = lax.fori_loop(0, n_sp, project, jnp.zeros((size, width), F32))
            packed = jnp.concatenate([total[:size // 2], total[size // 2:]], axis=1)
            rows = slice(start // 2, (start + size) // 2)
            psum_send[rows] = packed
            swap_copy(part).start()
            swap_copy(part).wait_recv()
            lat_mine[rows] = (packed + psum_recv[rows]).astype(BF16)

            def hand(step, carry, part=part):
                latent_copy(part, to_peer(step)).start()
                return carry

            lax.fori_loop(0, n_sp, hand, 0)

        turn_out(brl)

        for part in (0, 1):
            def handed(step, carry, part=part):
                latent_copy(part, to_peer(step)).wait_send()
                return carry

            lax.fori_loop(0, n_sp, handed, 0)
            swap_copy(part).wait_send()

    @pl.when(sec == 1)
    def _():
        lanes = lax.broadcasted_iota(jnp.int32, (tok, 2 * width), 1)

        def arrived(step, carry):
            branch_arrival(0, from_peer(step)).wait_recv()
            branch_arrival(1, from_peer(step)).wait_recv()
            return carry

        lax.fori_loop(1, n_sp, arrived, 0)
        picked = jnp.zeros((tok, 2 * width), F32)
        for part, onehot, table in ((0, onehot_a, lat_a), (1, onehot_b, lat_b)):
            def latent_in(step, carry, part=part):
                latent_arrival(part, from_peer(step)).wait_recv()
                return carry

            lax.fori_loop(0, n_sp, latent_in, 0)
            rows = table[...].reshape(n_sp * parts[part][1] // 2, 2 * width)
            low = jnp.dot(onehot[0], rows, preferred_element_type=F32)
            high = jnp.dot(onehot[1], rows, preferred_element_type=F32)
            picked = picked + jnp.where(lanes < width, low, high)
        wanted = picked.astype(BF16)

        def lift(g, carry):
            raised = jnp.dot(wanted, w2[g], preferred_element_type=F32)
            lifted[g] = (brl[g].astype(F32) + raised).astype(BF16)
            return carry

        lax.fori_loop(0, n_sp, lift, 0)
        turn_out(lifted)

    def drain(step, carry):
        target = to_peer(step)
        for c in (0, 1, 2):
            qkv_copy(c, target).wait_send()
        for part in (0, 1):
            branch_copy(part, target).wait_send()
        sibling_copy(target).wait_send()
        return carry

    lax.fori_loop(1, n_sp, drain, 0)
    sibling_copy(me).wait_send()


def on_device(qkv, counts, timesteps, block_map, w_out, w_in):
    n_sp = lax.axis_size("sp")
    tok, _, heads, hd = qkv.shape[2:]
    width = w_out.shape[2]
    seq = tok * n_sp
    half = tok // 2
    half_a = (tok // 32 // 2 * 32 + tok // 32 % 2 * 32) // 2
    dma = pltpu.SemaphoreType.DMA
    vmem = pl.BlockSpec(memory_space=pltpu.VMEM)
    hbm = pl.BlockSpec(memory_space=pltpu.HBM)

    def body(*refs):
        kernel(n_sp, tok, heads, hd, width, *refs)

    result = pl.pallas_call(
        body,
        name="guided_attention",
        out_shape=jax.ShapeDtypeStruct((tok, heads // 2, hd), BF16),
        in_specs=[hbm] * 6,
        out_specs=vmem,
        scratch_shapes=[
            pltpu.VMEM((3, tok, heads, hd), BF16),
            pltpu.VMEM((3, heads, tok, hd), BF16),
            pltpu.VMEM((n_sp, 2, tok, hd), BF16),
            pltpu.VMEM((2, seq, hd), BF16),
            pltpu.VMEM((2, seq, 2 * hd), BF16),
            pltpu.VMEM((2, hd, seq), BF16),
            pltpu.VMEM((2, tok, seq), F32),
            pltpu.VMEM((n_sp, tok, hd), BF16),
            pltpu.VMEM((n_sp, tok, hd), BF16),
            pltpu.VMEM((n_sp, tok, hd), BF16),
            pltpu.VMEM((n_sp, tok, hd), BF16),
            pltpu.VMEM((n_sp, tok, hd), BF16),
            pltpu.VMEM((half, 2 * width), BF16),
            pltpu.VMEM((n_sp, half_a, 2 * width), BF16),
            pltpu.VMEM((n_sp, half - half_a, 2 * width), BF16),
            pltpu.VMEM((half, 2 * width), F32),
            pltpu.VMEM((half, 2 * width), F32),
            pltpu.VMEM((2, tok, n_sp * half_a), BF16),
            pltpu.VMEM((2, tok, n_sp * (half - half_a)), BF16),
            pltpu.VMEM((heads, width, hd), BF16),
            pltpu.VMEM((width, heads, hd), BF16),
            pltpu.VMEM((heads // 2, 2 * width, hd), BF16),
            pltpu.VMEM((8, hd), F32),
            pltpu.VMEM((heads // 2, tok, hd), BF16),
            pltpu.SMEM((1, 1), jnp.int32),
            pltpu.SMEM((1, 1), jnp.int32),
            pltpu.VMEM((1, tok), jnp.int32),
            dma((3,)), dma((5,)), dma((3,)),
            dma((3, n_sp)), dma((3, n_sp)),
            dma((n_sp,)), dma((n_sp,)),
            dma((2, n_sp)), dma((2, n_sp)),
            dma((2,)), dma((2,)),
            dma((2, n_sp)), dma((2, n_sp)),
        ],
        compiler_params=pltpu.CompilerParams(
            collective_id=0, has_side_effects=True, vmem_limit_bytes=56 << 20
        ),
    )(
        qkv[0, 0],
        counts,
        timesteps,
        block_map.reshape(1, tok),
        jnp.swapaxes(w_out, 1, 2),
        w_in,
    )
    return result[None, :, None]


def solution(mesh):
    placed = (
        P("section", "cfg", ("req", "sp"), None, None, None),
        P("section", "req"),
        P("section", "req"),
        P(("req", "sp")),
        P(),
        P(),
    )
    return jax.shard_map(
        on_device,
        mesh=mesh,
        in_specs=placed,
        out_specs=P("section", ("req", "sp"), "cfg", None, None),
        check_vma=False,
    )
```

```python
import math

import jax
import jax.numpy as jnp
from jax import lax
from jax.experimental import pallas as pl
from jax.experimental.pallas import tpu as pltpu
from jax.sharding import PartitionSpec as P

MESH = pl.DeviceIdType.MESH
F32 = jnp.float32
BF16 = jnp.bfloat16
HOLD = 12
RELAYED = (1,)


def part_rows(tok):
    steps = tok // 32
    sizes = (32 * (steps * 3 // 5), 32 * (steps - 1 - steps * 3 // 5), 32)
    return tuple((sum(sizes[:n]), size) for n, size in enumerate(sizes))


def kernel(
    n_sp, tok, heads, hd, width,
    qkv_ref, cnt_ref, ts_ref, bm_ref, wo_ref, wi_ref, brl_out, wanted_out, w2_out,
    xin, stage, qland, kland, vaug, kt, sc, att_mine, att_send, att_recv, brs, brl, relay,
    lat_mine, lat_a, lat_b, lat_c, psum_send, psum_recv, onehot_a, onehot_b, onehot_c, wo, wi, gate,
    wanted_held, w2,
    cnt, ts, bm,
    in_sem, w_sem, own_sem, s_sem, r_sem, sib_s, sib_r, br_s, br_r, ps_s, ps_r, lat_s, lat_r,
    relay_s, relay_r, out_sem,
):
    seq = tok * n_sp
    parts = part_rows(tok)
    tables = (lat_a, lat_b, lat_c)
    onehots = (onehot_a, onehot_b, onehot_c)
    n_z = n_sp // 2
    sec = lax.axis_index("section")
    core = lax.axis_index("cfg")
    me = lax.axis_index("sp")
    scale = hd ** -0.5 * math.log2(math.e)

    def offset(step):
        turn = step // 2
        dz = ((turn + 1) // 2) * (1 - 2 * ((turn + 1) % 2))
        return step % 2, dz

    def to_peer(step):
        dx, dz = offset(step)
        return ((me // n_z + dx) % 2) * n_z + (me % n_z + dz + n_z) % n_z

    def query_peer(step):
        return from_peer(step)

    def from_peer(step):
        dx, dz = offset(step)
        return ((me // n_z + dx) % 2) * n_z + (me % n_z - dz + n_z) % n_z

    across = n_sp - 2
    mirror = (1 - me // n_z) * n_z + me % n_z
    mirror_opposite = (1 - me // n_z) * n_z + (me % n_z + n_z // 2) % n_z

    loads = [
        pltpu.make_async_copy(qkv_ref.at[:, c], xin.at[c], in_sem.at[c]) for c in (0, 1, 2)
    ]
    loads[1].start()
    smalls = [
        pltpu.make_async_copy(source, held, w_sem.at[n])
        for n, (source, held) in enumerate(
            ((wo_ref, wo), (wi_ref, wi), (cnt_ref, cnt), (ts_ref, ts), (bm_ref, bm))
        )
    ]

    barrier = pltpu.get_barrier_semaphore()

    def greet(step, carry):
        peer = to_peer(step)
        pl.semaphore_signal(barrier, inc=1, device_id={"sp": peer}, device_id_type=MESH)
        return carry

    lax.fori_loop(1, n_sp, greet, 0)
    pl.semaphore_signal(barrier, inc=1, device_id={"cfg": 1 - core}, device_id_type=MESH)
    for peer in (mirror, mirror_opposite):
        pl.semaphore_signal(
            barrier, inc=1, device_id={"section": 1 - sec, "sp": peer}, device_id_type=MESH
        )

    def transpose_kind(c):
        def body(t, carry):
            rows = pl.ds(pl.multiple_of(t * 16, 16), 16)
            stage[c, :, rows, :] = jnp.swapaxes(xin[c, rows], 0, 1)
            return carry

        lax.fori_loop(0, tok // 16, body, 0)

    def landing(c, source):
        if c == 0:
            return qland.at[source]
        rows = pl.ds(pl.multiple_of(source * tok, tok), tok)
        if c == 1:
            return kland.at[:, rows, :]
        return vaug.at[:, rows, pl.ds(0, hd)]

    def qkv_copy(c, target):
        return pltpu.make_async_remote_copy(
            src_ref=stage.at[c, pl.ds(2 * target, 2)],
            dst_ref=landing(c, me),
            send_sem=s_sem.at[c, target],
            recv_sem=r_sem.at[c, me],
            device_id={"sp": target},
            device_id_type=MESH,
        )

    def qkv_arrival(c, source):
        return pltpu.make_async_remote_copy(
            src_ref=stage.at[c, pl.ds(2 * source, 2)],
            dst_ref=landing(c, source),
            send_sem=s_sem.at[c, source],
            recv_sem=r_sem.at[c, source],
            device_id={"sp": source},
            device_id_type=MESH,
        )

    def own_copy(c):
        return pltpu.make_async_copy(
            stage.at[c, pl.ds(2 * me, 2)], landing(c, me), own_sem.at[c]
        )

    def send_kind(c):
        def body(step, carry):
            qkv_copy(c, to_peer(step)).start()
            return carry

        lax.fori_loop(1, n_sp, body, 0)
        own_copy(c).start()

    loads[1].wait()
    loads[2].start()
    loads[0].start()
    for small in smalls:
        small.start()
    transpose_kind(1)
    loads[2].wait()
    transpose_kind(2)
    pl.semaphore_wait(barrier, n_sp + 2)

    def to_relay(c):
        target = to_peer(across)
        return pltpu.make_async_remote_copy(
            src_ref=stage.at[c, pl.ds(2 * target, 2)],
            dst_ref=relay.at[c - 1],
            send_sem=s_sem.at[c, target],
            recv_sem=relay_r.at[c - 1],
            device_id={"section": 1, "sp": mirror},
            device_id_type=MESH,
        )

    def onward(c):
        return pltpu.make_async_remote_copy(
            src_ref=relay.at[c - 1],
            dst_ref=landing(c, mirror),
            send_sem=relay_s.at[c - 1],
            recv_sem=r_sem.at[c, mirror],
            device_id={"section": 0, "sp": mirror_opposite},
            device_id_type=MESH,
        )

    def relay_in(c):
        return pltpu.make_async_remote_copy(
            src_ref=relay.at[c - 1],
            dst_ref=relay.at[c - 1],
            send_sem=relay_s.at[c - 1],
            recv_sem=relay_r.at[c - 1],
            device_id={"section": 0, "sp": mirror},
            device_id_type=MESH,
        )

    def send_most(c):
        def body(step, carry):
            @pl.when(jnp.logical_or(sec == 1, step != across))
            def _():
                qkv_copy(c, to_peer(step)).start()

            return carry

        lax.fori_loop(1, n_sp, body, 0)
        own_copy(c).start()

    @pl.when(sec == 0)
    def _():
        for c in RELAYED:
            to_relay(c).start()

    (send_most if 1 in RELAYED else send_kind)(1)

    @pl.when(sec == 1)
    def _():
        for c in RELAYED:
            relay_in(c).wait_recv()
            onward(c).start()

    (send_most if 2 in RELAYED else send_kind)(2)
    loads[0].wait()
    transpose_kind(0)

    def send_query(step, carry):
        qkv_copy(0, to_peer(step)).start()
        return carry

    lax.fori_loop(1, n_sp, send_query, 0)
    own_copy(0).start()

    for small in smalls:
        small.wait()
    count = cnt[0, 0]
    head_id = (2 * me + core).astype(F32)
    dims = lax.broadcasted_iota(jnp.int32, (8, hd), 1).astype(F32)
    freq = jnp.exp(-math.log(10000.0) * dims / hd)
    gate[...] = 1.0 + 0.5 * jnp.sin(ts[0, 0].astype(F32) * freq + 0.7 * head_id)

    key_rows = lax.broadcasted_iota(jnp.int32, (seq, hd), 0)
    ones = jnp.where(key_rows < count, 1.0, 0.0).astype(BF16)
    vaug[0, :, hd:] = ones
    vaug[1, :, hd:] = ones

    for t in range(width // 16):
        stacked = jnp.swapaxes(wi[t * 16:t * 16 + 16], 0, 1).reshape(heads // 2, 2, 16, hd)
        chosen = jnp.where(core == 0, stacked[:, 0], stacked[:, 1])
        for g in range(heads // 2):
            for copy in (0, width):
                w2[copy + t * 16:copy + t * 16 + 16, g * hd:(g + 1) * hd] = chosen[g]

    w2_copy = pltpu.make_async_copy(w2, w2_out, out_sem.at[0])
    w2_copy.start()

    @pl.when(sec == 1)
    def _():
        eye = lax.broadcasted_iota(jnp.int32, (tok, tok), 0) == lax.broadcasted_iota(
            jnp.int32, (tok, tok), 1
        )
        wanted = jnp.sum(
            jnp.where(eye, jnp.broadcast_to(bm[...], (tok, tok)).astype(F32), 0.0),
            axis=1, keepdims=True,
        ).astype(jnp.int32)
        owner = wanted // tok
        row = wanted - owner * tok
        for onehot, (start, size) in zip(onehots, parts):
            depth = size // 2
            inside = row - start
            upper = (inside >= depth).astype(jnp.int32)
            slot = owner * depth + inside - upper * depth
            here = jnp.logical_and(inside >= 0, inside < size)
            places = lax.broadcasted_iota(jnp.int32, (tok, n_sp * depth), 1)
            for side in (0, 1):
                target = jnp.where(jnp.logical_and(here, upper == side), slot, -1)
                onehot[side] = jnp.where(places == target, 1.0, 0.0).astype(BF16)

    def wait_kind(c):
        def body(step, carry):
            qkv_arrival(c, from_peer(step)).wait_recv()
            return carry

        lax.fori_loop(1, n_sp, body, 0)
        own_copy(c).wait()

    quarter = seq // 4
    tail_ok = 3 * quarter + lax.broadcasted_iota(jnp.int32, (quarter, hd), 0) < count
    wait_kind(1)
    for h in (0, 1):
        for part in range(4):
            rows = slice(part * quarter, (part + 1) * quarter)
            block = kland[h, rows].astype(F32)
            if part == 3:
                block = jnp.where(tail_ok, block, kland[h, 0:16].astype(F32)[0:1])
            kt[h, :, rows] = block.T.astype(BF16)
    wait_kind(2)
    for h in (0, 1):
        tail = vaug[h, 3 * quarter:, :hd].astype(F32)
        vaug[h, 3 * quarter:, :hd] = jnp.where(tail_ok, tail, 0.0).astype(BF16)

    def sibling_copy(source):
        return pltpu.make_async_remote_copy(
            src_ref=att_send.at[source],
            dst_ref=att_recv.at[source],
            send_sem=sib_s.at[source],
            recv_sem=sib_r.at[source],
            device_id={"cfg": 1 - core},
            device_id_type=MESH,
        )

    def branch_copy(part, target):
        rows = pl.ds(*parts[part])
        return pltpu.make_async_remote_copy(
            src_ref=brs.at[target, rows],
            dst_ref=brl.at[me, rows],
            send_sem=br_s.at[part, target],
            recv_sem=br_r.at[part, me],
            device_id={"sp": target},
            device_id_type=MESH,
        )

    def branch_arrival(part, source):
        rows = pl.ds(*parts[part])
        return pltpu.make_async_remote_copy(
            src_ref=brs.at[source, rows],
            dst_ref=brl.at[source, rows],
            send_sem=br_s.at[part, source],
            recv_sem=br_r.at[part, source],
            device_id={"sp": source},
            device_id_type=MESH,
        )

    def attend(step):
        source = query_peer(step)
        for h in (0, 1):
            sc[h] = jnp.dot(qland[source, h], kt[h], preferred_element_type=F32)
        done = []
        for h in (0, 1):
            top = jnp.max(sc[h], axis=1, keepdims=True) * scale
            weights = jnp.exp2(sc[h] * scale - top).astype(BF16)
            mixed = jnp.dot(weights, vaug[h], preferred_element_type=F32)
            done.append(mixed[:, :hd] / mixed[:, hd:])
        att_mine[source] = jnp.where(core == 0, done[0], done[1]).astype(BF16)
        att_send[source] = jnp.where(core == 0, done[1], done[0]).astype(BF16)
        sibling_copy(source).start()

    def combine(step):
        source = query_peer(step)
        sibling_copy(source).wait_recv()
        mine = att_mine[source].astype(F32)
        theirs = att_recv[source].astype(F32)
        cond = jnp.where(core == 0, mine, theirs)
        uncond = jnp.where(core == 0, theirs, mine)
        guided = uncond + 5.0 * (cond - uncond)
        position = source * tok + lax.broadcasted_iota(jnp.int32, (tok, hd), 0)
        return source, jnp.where(position < count, gate[0:1] * guided, 0.0).astype(BF16)

    def keep(step):
        target, block = combine(step)
        brs[target] = block

    def send_part(part, step):
        branch_copy(part, query_peer(step)).start()

    own_copy(0).wait()
    attend(0)

    def first(step, carry):
        qkv_arrival(0, query_peer(step)).wait_recv()
        attend(step)

        @pl.when(step == 1)
        def _():
            source, block = combine(0)
            brl[source] = block

        @pl.when(step > 1)
        def _():
            keep(step - 1)

        return carry

    def release(step, carry):
        send_part(0, step)
        return carry

    def later(step, carry):
        qkv_arrival(0, query_peer(step)).wait_recv()
        attend(step)
        keep(step - 1)
        send_part(0, step - 1)
        return carry

    hold = n_sp - 1 if n_sp < HOLD else HOLD
    lax.fori_loop(1, hold, first, 0)
    lax.fori_loop(1, hold - 1, release, 0)
    lax.fori_loop(hold, n_sp, later, 0)
    keep(n_sp - 1)
    send_part(0, n_sp - 1)

    for part in range(1, len(parts)):
        def send_rest(step, carry, part=part):
            send_part(part, step)
            return carry

        lax.fori_loop(1, n_sp, send_rest, 0)

    def swap_copy(part):
        rows = pl.ds(parts[part][0] // 2, parts[part][1] // 2)
        return pltpu.make_async_remote_copy(
            src_ref=psum_send.at[rows], dst_ref=psum_recv.at[rows],
            send_sem=ps_s.at[part], recv_sem=ps_r.at[part],
            device_id={"cfg": 1 - core}, device_id_type=MESH,
        )

    def latent_copy(part, target):
        rows = pl.ds(parts[part][0] // 2, parts[part][1] // 2)
        return pltpu.make_async_remote_copy(
            src_ref=lat_mine.at[rows], dst_ref=tables[part].at[me],
            send_sem=lat_s.at[part, target], recv_sem=lat_r.at[part, me],
            device_id={"section": 1, "sp": target}, device_id_type=MESH,
        )

    def latent_arrival(part, source):
        rows = pl.ds(parts[part][0] // 2, parts[part][1] // 2)
        return pltpu.make_async_remote_copy(
            src_ref=lat_mine.at[rows], dst_ref=tables[part].at[source],
            send_sem=lat_s.at[part, source], recv_sem=lat_r.at[part, source],
            device_id={"section": 0, "sp": source}, device_id_type=MESH,
        )

    def drain(step, carry):
        target = to_peer(step)
        for c in (0, 1, 2):
            qkv_copy(c, target).wait_send()
        sibling_copy(target).wait_send()
        return carry

    lax.fori_loop(1, n_sp, drain, 0)
    sibling_copy(me).wait_send()

    def drain_branch(step, carry):
        for part in range(len(parts)):
            branch_copy(part, to_peer(step)).wait_send()
        return carry

    wanted_copy = pltpu.make_async_copy(wanted_held, wanted_out, out_sem.at[1])
    brl_copy = pltpu.make_async_copy(brl, brl_out, out_sem.at[2])

    @pl.when(sec == 0)
    def _():
        for part, (start, size) in enumerate(parts):
            def returned(step, carry, part=part):
                branch_arrival(part, from_peer(step)).wait_recv()
                return carry

            lax.fori_loop(1, n_sp, returned, 0)
            total = jnp.zeros((size, width), F32)
            for source in range(n_sp):
                total = total + lax.dot_general(
                    brl[source, start:start + size], wo[2 * source + core],
                    (((1,), (1,)), ((), ())), preferred_element_type=F32,
                )
            packed = jnp.concatenate([total[:size // 2], total[size // 2:]], axis=1)
            rows = slice(start // 2, (start + size) // 2)
            psum_send[rows] = packed
            swap_copy(part).start()
            swap_copy(part).wait_recv()
            lat_mine[rows] = (packed + psum_recv[rows]).astype(BF16)

            def hand(step, carry, part=part):
                latent_copy(part, to_peer(step)).start()
                return carry

            lax.fori_loop(0, n_sp, hand, 0)

        wanted_held[...] = jnp.zeros_like(wanted_held)
        wanted_copy.start()
        brl_copy.start()
        lax.fori_loop(1, n_sp, drain_branch, 0)
        for part in range(len(parts)):
            def handed(step, carry, part=part):
                latent_copy(part, to_peer(step)).wait_send()
                return carry

            lax.fori_loop(0, n_sp, handed, 0)
            swap_copy(part).wait_send()

    @pl.when(sec == 1)
    def _():
        lanes = lax.broadcasted_iota(jnp.int32, (tok, 2 * width), 1)

        def arrived(step, carry):
            for part in range(len(parts)):
                branch_arrival(part, from_peer(step)).wait_recv()
            return carry

        lax.fori_loop(1, n_sp, arrived, 0)
        brl_copy.start()
        lax.fori_loop(1, n_sp, drain_branch, 0)
        picked = jnp.zeros((tok, 2 * width), F32)
        for part, (onehot, table) in enumerate(zip(onehots, tables)):
            def latent_in(step, carry, part=part):
                latent_arrival(part, from_peer(step)).wait_recv()
                return carry

            lax.fori_loop(0, n_sp, latent_in, 0)
            rows = table[...].reshape(n_sp * parts[part][1] // 2, 2 * width)
            low = jnp.dot(onehot[0], rows, preferred_element_type=F32)
            high = jnp.dot(onehot[1], rows, preferred_element_type=F32)
            picked = picked + jnp.where(lanes < width, low, high)
        wanted_held[...] = picked.astype(BF16)
        wanted_copy.start()

    w2_copy.wait()
    brl_copy.wait()
    wanted_copy.wait()

    @pl.when(sec == 1)
    def _():
        for c in RELAYED:
            onward(c).wait_send()


def lift_kernel(wanted_ref, w2_ref, brl_ref, out_ref):
    groups, _, hd = brl_ref.shape
    raised = jnp.dot(wanted_ref[...], w2_ref[...], preferred_element_type=F32)
    result = jnp.stack(
        [
            (brl_ref[g].astype(F32) + raised[:, g * hd:(g + 1) * hd]).astype(BF16)
            for g in range(groups)
        ]
    )
    out_ref[...] = jnp.swapaxes(result, 0, 1)


def on_device(qkv, counts, timesteps, block_map, w_out, w_in):
    n_sp = lax.axis_size("sp")
    tok, _, heads, hd = qkv.shape[2:]
    width = w_out.shape[2]
    seq = tok * n_sp
    half = tok // 2
    halves = [size // 2 for _, size in part_rows(tok)]
    dma = pltpu.SemaphoreType.DMA
    hbm = pl.BlockSpec(memory_space=pltpu.HBM)

    def body(*refs):
        kernel(n_sp, tok, heads, hd, width, *refs)

    brl, wanted, w2 = pl.pallas_call(
        body,
        name="guided_attention",
        out_shape=(
            jax.ShapeDtypeStruct((n_sp, tok, hd), BF16),
            jax.ShapeDtypeStruct((tok, 2 * width), BF16),
            jax.ShapeDtypeStruct((2 * width, heads // 2 * hd), BF16),
        ),
        in_specs=[hbm] * 6,
        out_specs=(hbm, hbm, hbm),
        scratch_shapes=[
            pltpu.VMEM((3, tok, heads, hd), BF16),
            pltpu.VMEM((3, heads, tok, hd), BF16),
            pltpu.VMEM((n_sp, 2, tok, hd), BF16),
            pltpu.VMEM((2, seq, hd), BF16),
            pltpu.VMEM((2, seq, 2 * hd), BF16),
            pltpu.VMEM((2, hd, seq), BF16),
            pltpu.VMEM((2, tok, seq), F32),
            pltpu.VMEM((n_sp, tok, hd), BF16),
            pltpu.VMEM((n_sp, tok, hd), BF16),
            pltpu.VMEM((n_sp, tok, hd), BF16),
            pltpu.VMEM((n_sp, tok, hd), BF16),
            pltpu.VMEM((n_sp, tok, hd), BF16),
            pltpu.VMEM((2, 2, tok, hd), BF16),
            pltpu.VMEM((half, 2 * width), BF16),
            *[pltpu.VMEM((n_sp, depth, 2 * width), BF16) for depth in halves],
            pltpu.VMEM((half, 2 * width), F32),
            pltpu.VMEM((half, 2 * width), F32),
            *[pltpu.VMEM((2, tok, n_sp * depth), BF16) for depth in halves],
            pltpu.VMEM((heads, width, hd), BF16),
            pltpu.VMEM((width, heads, hd), BF16),
            pltpu.VMEM((8, hd), F32),
            pltpu.VMEM((tok, 2 * width), BF16),
            pltpu.VMEM((2 * width, heads // 2 * hd), BF16),
            pltpu.SMEM((1, 1), jnp.int32),
            pltpu.SMEM((1, 1), jnp.int32),
            pltpu.VMEM((1, tok), jnp.int32),
            dma((3,)), dma((5,)), dma((3,)),
            dma((3, n_sp)), dma((3, n_sp)),
            dma((n_sp,)), dma((n_sp,)),
            dma((3, n_sp)), dma((3, n_sp)),
            dma((3,)), dma((3,)),
            dma((3, n_sp)), dma((3, n_sp)),
            dma((2,)), dma((2,)), dma((3,)),
        ],
        compiler_params=pltpu.CompilerParams(
            collective_id=0, has_side_effects=True, vmem_limit_bytes=56 << 20
        ),
    )(
        qkv[0, 0],
        counts,
        timesteps,
        block_map.reshape(1, tok),
        jnp.swapaxes(w_out, 1, 2),
        w_in,
    )
    result = pl.pallas_call(
        lift_kernel,
        name="lift",
        out_shape=jax.ShapeDtypeStruct((tok, heads // 2, hd), BF16),
    )(wanted, w2, brl)
    return result[None, :, None]


def solution(mesh):
    placed = (
        P("section", "cfg", ("req", "sp"), None, None, None),
        P("section", "req"),
        P("section", "req"),
        P(("req", "sp")),
        P(),
        P(),
    )
    return jax.shard_map(
        on_device,
        mesh=mesh,
        in_specs=placed,
        out_specs=P("section", ("req", "sp"), "cfg", None, None),
        check_vma=False,
    )
```

```python
import math

import jax
import jax.numpy as jnp
from jax import lax
from jax.experimental import pallas as pl
from jax.experimental.pallas import tpu as pltpu
from jax.sharding import PartitionSpec as P

MESH = pl.DeviceIdType.MESH
F32 = jnp.float32
BF16 = jnp.bfloat16
HOLD = 12
RELAYED = (1,)


def part_rows(tok):
    steps = tok // 32
    sizes = (32 * (steps * 3 // 5), 32 * (steps - 1 - steps * 3 // 5), 32)
    return tuple((sum(sizes[:n]), size) for n, size in enumerate(sizes))


def kernel(
    n_sp, tok, heads, hd, width,
    qkv_ref, cnt_ref, ts_ref, bm_ref, wo_ref, wi_ref, brl_out, wanted_out, w2_out,
    xin, stage, qland, kland, vaug, kt, sc, att_mine, att_send, att_recv, brs, brl, relay,
    lat_mine, lat_a, lat_b, lat_c, psum_send, psum_recv, onehot_a, onehot_b, onehot_c, wo, wi, gate,
    wanted_held, w2,
    cnt, ts, bm,
    in_sem, w_sem, own_sem, s_sem, r_sem, q_sem, sib_s, sib_r, br_s, br_r, ps_s, ps_r, lat_s, lat_r,
    relay_s, relay_r, out_sem,
):
    seq = tok * n_sp
    parts = part_rows(tok)
    tables = (lat_a, lat_b, lat_c)
    onehots = (onehot_a, onehot_b, onehot_c)
    n_z = n_sp // 2
    sec = lax.axis_index("section")
    core = lax.axis_index("cfg")
    me = lax.axis_index("sp")
    scale = hd ** -0.5 * math.log2(math.e)

    def offset(step):
        turn = step // 2
        dz = ((turn + 1) // 2) * (1 - 2 * ((turn + 1) % 2))
        return step % 2, dz

    def to_peer(step):
        dx, dz = offset(step)
        return ((me // n_z + dx) % 2) * n_z + (me % n_z + dz + n_z) % n_z

    def query_peer(step):
        return from_peer(step)

    def from_peer(step):
        dx, dz = offset(step)
        return ((me // n_z + dx) % 2) * n_z + (me % n_z - dz + n_z) % n_z

    across = n_sp - 2
    mirror = (1 - me // n_z) * n_z + me % n_z
    mirror_opposite = (1 - me // n_z) * n_z + (me % n_z + n_z // 2) % n_z

    loads = [
        pltpu.make_async_copy(qkv_ref.at[:, c], xin.at[c], in_sem.at[c]) for c in (0, 1, 2)
    ]
    loads[1].start()
    smalls = [
        pltpu.make_async_copy(source, held, w_sem.at[n])
        for n, (source, held) in enumerate(
            ((wo_ref, wo), (wi_ref, wi), (cnt_ref, cnt), (ts_ref, ts), (bm_ref, bm))
        )
    ]

    barrier = pltpu.get_barrier_semaphore()

    def greet(step, carry):
        peer = to_peer(step)
        pl.semaphore_signal(barrier, inc=1, device_id={"sp": peer}, device_id_type=MESH)
        return carry

    lax.fori_loop(1, n_sp, greet, 0)
    pl.semaphore_signal(barrier, inc=1, device_id={"cfg": 1 - core}, device_id_type=MESH)
    for peer in (mirror, mirror_opposite):
        pl.semaphore_signal(
            barrier, inc=1, device_id={"section": 1 - sec, "sp": peer}, device_id_type=MESH
        )

    def transpose_kind(c):
        def body(t, carry):
            rows = pl.ds(pl.multiple_of(t * 16, 16), 16)
            stage[c, :, rows, :] = jnp.swapaxes(xin[c, rows], 0, 1)
            return carry

        lax.fori_loop(0, tok // 16, body, 0)

    def landing(c, source):
        if c == 0:
            return qland.at[source]
        rows = pl.ds(pl.multiple_of(source * tok, tok), tok)
        if c == 1:
            return kland.at[:, rows, :]
        return vaug.at[:, rows, pl.ds(0, hd)]

    def qkv_copy(c, target):
        return pltpu.make_async_remote_copy(
            src_ref=stage.at[c, pl.ds(2 * target, 2)],
            dst_ref=landing(c, me),
            send_sem=s_sem.at[c],
            recv_sem=q_sem.at[me] if c == 0 else r_sem.at[c],
            device_id={"sp": target},
            device_id_type=MESH,
        )

    def query_arrival(source):
        return pltpu.make_async_remote_copy(
            src_ref=qland.at[source],
            dst_ref=qland.at[source],
            send_sem=s_sem.at[0],
            recv_sem=q_sem.at[source],
            device_id={"sp": source},
            device_id_type=MESH,
        )

    def all_sent(held, sem):
        pltpu.make_async_remote_copy(
            src_ref=held, dst_ref=held, send_sem=sem, recv_sem=sem,
            device_id={"cfg": 1 - core}, device_id_type=MESH,
        ).wait_send()

    def all_arrived(held, sem):
        pltpu.make_async_remote_copy(
            src_ref=held, dst_ref=held, send_sem=sem, recv_sem=sem,
            device_id={"cfg": 1 - core}, device_id_type=MESH,
        ).wait_recv()

    def own_copy(c):
        return pltpu.make_async_copy(
            stage.at[c, pl.ds(2 * me, 2)], landing(c, me), own_sem.at[c]
        )

    def send_kind(c):
        def body(step, carry):
            qkv_copy(c, to_peer(step)).start()
            return carry

        lax.fori_loop(1, n_sp, body, 0)
        own_copy(c).start()

    loads[1].wait()
    loads[2].start()
    loads[0].start()
    for small in smalls:
        small.start()
    transpose_kind(1)
    loads[2].wait()
    transpose_kind(2)
    pl.semaphore_wait(barrier, n_sp + 2)

    def to_relay(c):
        target = to_peer(across)
        return pltpu.make_async_remote_copy(
            src_ref=stage.at[c, pl.ds(2 * target, 2)],
            dst_ref=relay.at[c - 1],
            send_sem=s_sem.at[c],
            recv_sem=relay_r.at[c - 1],
            device_id={"section": 1, "sp": mirror},
            device_id_type=MESH,
        )

    def onward(c):
        return pltpu.make_async_remote_copy(
            src_ref=relay.at[c - 1],
            dst_ref=landing(c, mirror),
            send_sem=relay_s.at[c - 1],
            recv_sem=r_sem.at[c],
            device_id={"section": 0, "sp": mirror_opposite},
            device_id_type=MESH,
        )

    def relay_in(c):
        return pltpu.make_async_remote_copy(
            src_ref=relay.at[c - 1],
            dst_ref=relay.at[c - 1],
            send_sem=relay_s.at[c - 1],
            recv_sem=relay_r.at[c - 1],
            device_id={"section": 0, "sp": mirror},
            device_id_type=MESH,
        )

    def send_most(c):
        def body(step, carry):
            @pl.when(jnp.logical_or(sec == 1, step != across))
            def _():
                qkv_copy(c, to_peer(step)).start()

            return carry

        lax.fori_loop(1, n_sp, body, 0)
        own_copy(c).start()

    @pl.when(sec == 0)
    def _():
        for c in RELAYED:
            to_relay(c).start()

    (send_most if 1 in RELAYED else send_kind)(1)

    @pl.when(sec == 1)
    def _():
        for c in RELAYED:
            relay_in(c).wait_recv()
            onward(c).start()

    (send_most if 2 in RELAYED else send_kind)(2)
    loads[0].wait()
    transpose_kind(0)

    def send_query(step, carry):
        qkv_copy(0, to_peer(step)).start()
        return carry

    lax.fori_loop(1, n_sp, send_query, 0)
    own_copy(0).start()

    for small in smalls:
        small.wait()
    count = cnt[0, 0]
    head_id = (2 * me + core).astype(F32)
    dims = lax.broadcasted_iota(jnp.int32, (8, hd), 1).astype(F32)
    freq = jnp.exp(-math.log(10000.0) * dims / hd)
    gate[...] = 1.0 + 0.5 * jnp.sin(ts[0, 0].astype(F32) * freq + 0.7 * head_id)

    key_rows = lax.broadcasted_iota(jnp.int32, (seq, hd), 0)
    ones = jnp.where(key_rows < count, 1.0, 0.0).astype(BF16)
    vaug[0, :, hd:] = ones
    vaug[1, :, hd:] = ones

    for t in range(width // 16):
        stacked = jnp.swapaxes(wi[t * 16:t * 16 + 16], 0, 1).reshape(heads // 2, 2, 16, hd)
        chosen = jnp.where(core == 0, stacked[:, 0], stacked[:, 1])
        for g in range(heads // 2):
            for copy in (0, width):
                w2[copy + t * 16:copy + t * 16 + 16, g * hd:(g + 1) * hd] = chosen[g]

    w2_copy = pltpu.make_async_copy(w2, w2_out, out_sem.at[0])
    w2_copy.start()

    @pl.when(sec == 1)
    def _():
        eye = lax.broadcasted_iota(jnp.int32, (tok, tok), 0) == lax.broadcasted_iota(
            jnp.int32, (tok, tok), 1
        )
        wanted = jnp.sum(
            jnp.where(eye, jnp.broadcast_to(bm[...], (tok, tok)).astype(F32), 0.0),
            axis=1, keepdims=True,
        ).astype(jnp.int32)
        owner = wanted // tok
        row = wanted - owner * tok
        for onehot, (start, size) in zip(onehots, parts):
            depth = size // 2
            inside = row - start
            upper = (inside >= depth).astype(jnp.int32)
            slot = owner * depth + inside - upper * depth
            here = jnp.logical_and(inside >= 0, inside < size)
            places = lax.broadcasted_iota(jnp.int32, (tok, n_sp * depth), 1)
            for side in (0, 1):
                target = jnp.where(jnp.logical_and(here, upper == side), slot, -1)
                onehot[side] = jnp.where(places == target, 1.0, 0.0).astype(BF16)

    others = pl.ds(0, (n_sp - 1) * tok)

    def wait_kind(c):
        all_arrived(
            kland.at[:, others] if c == 1 else vaug.at[:, others, pl.ds(0, hd)], r_sem.at[c]
        )
        own_copy(c).wait()

    quarter = seq // 4
    tail_ok = 3 * quarter + lax.broadcasted_iota(jnp.int32, (quarter, hd), 0) < count
    wait_kind(1)
    for h in (0, 1):
        for part in range(4):
            rows = slice(part * quarter, (part + 1) * quarter)
            block = kland[h, rows].astype(F32)
            if part == 3:
                block = jnp.where(tail_ok, block, kland[h, 0:16].astype(F32)[0:1])
            kt[h, :, rows] = block.T.astype(BF16)
    wait_kind(2)
    for h in (0, 1):
        tail = vaug[h, 3 * quarter:, :hd].astype(F32)
        vaug[h, 3 * quarter:, :hd] = jnp.where(tail_ok, tail, 0.0).astype(BF16)

    def sibling_copy(source):
        return pltpu.make_async_remote_copy(
            src_ref=att_send.at[source],
            dst_ref=att_recv.at[source],
            send_sem=sib_s,
            recv_sem=sib_r.at[source],
            device_id={"cfg": 1 - core},
            device_id_type=MESH,
        )

    def branch_copy(part, target):
        rows = pl.ds(*parts[part])
        return pltpu.make_async_remote_copy(
            src_ref=brs.at[target, rows],
            dst_ref=brl.at[me, rows],
            send_sem=br_s.at[part],
            recv_sem=br_r.at[part],
            device_id={"sp": target},
            device_id_type=MESH,
        )

    def branches(blocks, part):
        return blocks.at[pl.ds(0, n_sp - 1), pl.ds(*parts[part])]

    def attend(step):
        source = query_peer(step)
        for h in (0, 1):
            sc[h] = jnp.dot(qland[source, h], kt[h], preferred_element_type=F32)
        done = []
        for h in (0, 1):
            top = jnp.max(sc[h], axis=1, keepdims=True) * scale
            weights = jnp.exp2(sc[h] * scale - top).astype(BF16)
            mixed = jnp.dot(weights, vaug[h], preferred_element_type=F32)
            done.append(mixed[:, :hd] / mixed[:, hd:])
        att_mine[source] = jnp.where(core == 0, done[0], done[1]).astype(BF16)
        att_send[source] = jnp.where(core == 0, done[1], done[0]).astype(BF16)
        sibling_copy(source).start()

    def combine(step):
        source = query_peer(step)
        sibling_copy(source).wait_recv()
        mine = att_mine[source].astype(F32)
        theirs = att_recv[source].astype(F32)
        cond = jnp.where(core == 0, mine, theirs)
        uncond = jnp.where(core == 0, theirs, mine)
        guided = uncond + 5.0 * (cond - uncond)
        position = source * tok + lax.broadcasted_iota(jnp.int32, (tok, hd), 0)
        return source, jnp.where(position < count, gate[0:1] * guided, 0.0).astype(BF16)

    def keep(step):
        target, block = combine(step)
        brs[target] = block

    def send_part(part, step):
        branch_copy(part, query_peer(step)).start()

    own_copy(0).wait()
    attend(0)

    def first(step, carry):
        query_arrival(query_peer(step)).wait_recv()
        attend(step)

        @pl.when(step == 1)
        def _():
            source, block = combine(0)
            brl[source] = block

        @pl.when(step > 1)
        def _():
            keep(step - 1)

        return carry

    def release(step, carry):
        send_part(0, step)
        return carry

    def later(step, carry):
        query_arrival(query_peer(step)).wait_recv()
        attend(step)
        keep(step - 1)
        send_part(0, step - 1)
        return carry

    hold = n_sp - 1 if n_sp < HOLD else HOLD
    lax.fori_loop(1, hold, first, 0)
    lax.fori_loop(1, hold - 1, release, 0)
    lax.fori_loop(hold, n_sp, later, 0)
    keep(n_sp - 1)
    send_part(0, n_sp - 1)

    for part in range(1, len(parts)):
        def send_rest(step, carry, part=part):
            send_part(part, step)
            return carry

        lax.fori_loop(1, n_sp, send_rest, 0)

    def swap_copy(part):
        rows = pl.ds(parts[part][0] // 2, parts[part][1] // 2)
        return pltpu.make_async_remote_copy(
            src_ref=psum_send.at[rows], dst_ref=psum_recv.at[rows],
            send_sem=ps_s.at[part], recv_sem=ps_r.at[part],
            device_id={"cfg": 1 - core}, device_id_type=MESH,
        )

    def latent_copy(part, target):
        rows = pl.ds(parts[part][0] // 2, parts[part][1] // 2)
        return pltpu.make_async_remote_copy(
            src_ref=lat_mine.at[rows], dst_ref=tables[part].at[me],
            send_sem=lat_s.at[part], recv_sem=lat_r.at[part],
            device_id={"section": 1, "sp": target}, device_id_type=MESH,
        )

    for c in (0, 1, 2):
        all_sent(stage.at[c, pl.ds(0, 2 * (n_sp - 1))], s_sem.at[c])
    all_sent(att_send, sib_s)

    wanted_copy = pltpu.make_async_copy(wanted_held, wanted_out, out_sem.at[1])
    brl_copy = pltpu.make_async_copy(brl, brl_out, out_sem.at[2])

    @pl.when(sec == 0)
    def _():
        for part, (start, size) in enumerate(parts):
            all_arrived(branches(brl, part), br_r.at[part])
            total = jnp.zeros((size, width), F32)
            for source in range(n_sp):
                total = total + lax.dot_general(
                    brl[source, start:start + size], wo[2 * source + core],
                    (((1,), (1,)), ((), ())), preferred_element_type=F32,
                )
            packed = jnp.concatenate([total[:size // 2], total[size // 2:]], axis=1)
            rows = slice(start // 2, (start + size) // 2)
            psum_send[rows] = packed
            swap_copy(part).start()
            swap_copy(part).wait_recv()
            lat_mine[rows] = (packed + psum_recv[rows]).astype(BF16)

            def hand(step, carry, part=part):
                latent_copy(part, to_peer(step)).start()
                return carry

            lax.fori_loop(0, n_sp, hand, 0)

        wanted_held[...] = jnp.zeros_like(wanted_held)
        wanted_copy.start()
        brl_copy.start()
        for part in range(len(parts)):
            all_sent(branches(brs, part), br_s.at[part])
            all_sent(tables[part], lat_s.at[part])
            swap_copy(part).wait_send()

    @pl.when(sec == 1)
    def _():
        lanes = lax.broadcasted_iota(jnp.int32, (tok, 2 * width), 1)

        for part in range(len(parts)):
            all_arrived(branches(brl, part), br_r.at[part])
        brl_copy.start()
        for part in range(len(parts)):
            all_sent(branches(brs, part), br_s.at[part])
        picked = jnp.zeros((tok, 2 * width), F32)
        for part, (onehot, table) in enumerate(zip(onehots, tables)):
            all_arrived(table, lat_r.at[part])
            rows = table[...].reshape(n_sp * parts[part][1] // 2, 2 * width)
            low = jnp.dot(onehot[0], rows, preferred_element_type=F32)
            high = jnp.dot(onehot[1], rows, preferred_element_type=F32)
            picked = picked + jnp.where(lanes < width, low, high)
        wanted_held[...] = picked.astype(BF16)
        wanted_copy.start()

    w2_copy.wait()
    brl_copy.wait()
    wanted_copy.wait()

    @pl.when(sec == 1)
    def _():
        for c in RELAYED:
            onward(c).wait_send()


def lift_kernel(wanted_ref, w2_ref, brl_ref, out_ref):
    groups, _, hd = brl_ref.shape
    raised = jnp.dot(wanted_ref[...], w2_ref[...], preferred_element_type=F32)
    result = jnp.stack(
        [
            (brl_ref[g].astype(F32) + raised[:, g * hd:(g + 1) * hd]).astype(BF16)
            for g in range(groups)
        ]
    )
    out_ref[...] = jnp.swapaxes(result, 0, 1)


def on_device(qkv, counts, timesteps, block_map, w_out, w_in):
    n_sp = lax.axis_size("sp")
    tok, _, heads, hd = qkv.shape[2:]
    width = w_out.shape[2]
    seq = tok * n_sp
    half = tok // 2
    halves = [size // 2 for _, size in part_rows(tok)]
    dma = pltpu.SemaphoreType.DMA
    hbm = pl.BlockSpec(memory_space=pltpu.HBM)

    def body(*refs):
        kernel(n_sp, tok, heads, hd, width, *refs)

    brl, wanted, w2 = pl.pallas_call(
        body,
        name="guided_attention",
        out_shape=(
            jax.ShapeDtypeStruct((n_sp, tok, hd), BF16),
            jax.ShapeDtypeStruct((tok, 2 * width), BF16),
            jax.ShapeDtypeStruct((2 * width, heads // 2 * hd), BF16),
        ),
        in_specs=[hbm] * 6,
        out_specs=(hbm, hbm, hbm),
        scratch_shapes=[
            pltpu.VMEM((3, tok, heads, hd), BF16),
            pltpu.VMEM((3, heads, tok, hd), BF16),
            pltpu.VMEM((n_sp, 2, tok, hd), BF16),
            pltpu.VMEM((2, seq, hd), BF16),
            pltpu.VMEM((2, seq, 2 * hd), BF16),
            pltpu.VMEM((2, hd, seq), BF16),
            pltpu.VMEM((2, tok, seq), F32),
            pltpu.VMEM((n_sp, tok, hd), BF16),
            pltpu.VMEM((n_sp, tok, hd), BF16),
            pltpu.VMEM((n_sp, tok, hd), BF16),
            pltpu.VMEM((n_sp, tok, hd), BF16),
            pltpu.VMEM((n_sp, tok, hd), BF16),
            pltpu.VMEM((2, 2, tok, hd), BF16),
            pltpu.VMEM((half, 2 * width), BF16),
            *[pltpu.VMEM((n_sp, depth, 2 * width), BF16) for depth in halves],
            pltpu.VMEM((half, 2 * width), F32),
            pltpu.VMEM((half, 2 * width), F32),
            *[pltpu.VMEM((2, tok, n_sp * depth), BF16) for depth in halves],
            pltpu.VMEM((heads, width, hd), BF16),
            pltpu.VMEM((width, heads, hd), BF16),
            pltpu.VMEM((8, hd), F32),
            pltpu.VMEM((tok, 2 * width), BF16),
            pltpu.VMEM((2 * width, heads // 2 * hd), BF16),
            pltpu.SMEM((1, 1), jnp.int32),
            pltpu.SMEM((1, 1), jnp.int32),
            pltpu.VMEM((1, tok), jnp.int32),
            dma((3,)), dma((5,)), dma((3,)),
            dma((3,)), dma((3,)), dma((n_sp,)),
            dma, dma((n_sp,)),
            dma((3,)), dma((3,)),
            dma((3,)), dma((3,)),
            dma((3,)), dma((3,)),
            dma((2,)), dma((2,)), dma((3,)),
        ],
        compiler_params=pltpu.CompilerParams(
            collective_id=0, has_side_effects=True, vmem_limit_bytes=56 << 20
        ),
    )(
        qkv[0, 0],
        counts,
        timesteps,
        block_map.reshape(1, tok),
        jnp.swapaxes(w_out, 1, 2),
        w_in,
    )
    result = pl.pallas_call(
        lift_kernel,
        name="lift",
        out_shape=jax.ShapeDtypeStruct((tok, heads // 2, hd), BF16),
    )(wanted, w2, brl)
    return result[None, :, None]


def solution(mesh):
    placed = (
        P("section", "cfg", ("req", "sp"), None, None, None),
        P("section", "req"),
        P("section", "req"),
        P(("req", "sp")),
        P(),
        P(),
    )
    return jax.shard_map(
        on_device,
        mesh=mesh,
        in_specs=placed,
        out_specs=P("section", ("req", "sp"), "cfg", None, None),
        check_vma=False,
    )
```

```python
import math

import jax
import jax.numpy as jnp
from jax import lax
from jax.experimental import pallas as pl
from jax.experimental.pallas import tpu as pltpu
from jax.sharding import PartitionSpec as P

MESH = pl.DeviceIdType.MESH
F32 = jnp.float32
BF16 = jnp.bfloat16
HOLD = 12
RELAYED = (1,)


def part_rows(tok):
    steps = tok // 32
    sizes = (32 * (steps * 3 // 5), 32 * (steps - 1 - steps * 3 // 5), 32)
    return tuple((sum(sizes[:n]), size) for n, size in enumerate(sizes))


def kernel(
    n_sp, tok, heads, hd, width,
    qkv_ref, cnt_ref, ts_ref, bm_ref, wo_ref, wi_ref, brl_out, wanted_out, w2_out,
    xin, stage, qland, kland, vaug, kt, sc, att_mine, att_send, att_recv, brs, brl, relay,
    lat_mine, lat_a, lat_b, lat_c, psum_send, psum_recv, onehot_a, onehot_b, onehot_c, wo, wi, gate,
    wanted_held, w2,
    cnt, ts, bm,
    in_sem, w_sem, own_sem, s_sem, r_sem, q_sem, sib_s, sib_r, br_s, br_r, ps_s, ps_r, lat_s, lat_r,
    relay_s, relay_r, out_sem,
):
    seq = tok * n_sp
    parts = part_rows(tok)
    tables = (lat_a, lat_b, lat_c)
    onehots = (onehot_a, onehot_b, onehot_c)
    n_z = n_sp // 2
    sec = lax.axis_index("section")
    core = lax.axis_index("cfg")
    me = lax.axis_index("sp")
    scale = hd ** -0.5 * math.log2(math.e)

    def offset(step):
        turn = step // 2
        dz = ((turn + 1) // 2) * (1 - 2 * ((turn + 1) % 2))
        return step % 2, dz

    def to_peer(step):
        dx, dz = offset(step)
        return ((me // n_z + dx) % 2) * n_z + (me % n_z + dz + n_z) % n_z

    def query_peer(step):
        return from_peer(step)

    def from_peer(step):
        dx, dz = offset(step)
        return ((me // n_z + dx) % 2) * n_z + (me % n_z - dz + n_z) % n_z

    across = n_sp - 2
    mirror = (1 - me // n_z) * n_z + me % n_z
    mirror_opposite = (1 - me // n_z) * n_z + (me % n_z + n_z // 2) % n_z

    loads = [
        pltpu.make_async_copy(qkv_ref.at[:, c], xin.at[c], in_sem.at[c]) for c in (0, 1, 2)
    ]
    loads[1].start()
    smalls = [
        pltpu.make_async_copy(source, held, w_sem.at[n])
        for n, (source, held) in enumerate(
            ((wo_ref, wo), (wi_ref, wi), (cnt_ref, cnt), (ts_ref, ts), (bm_ref, bm))
        )
    ]

    barrier = pltpu.get_barrier_semaphore()

    def greet(step, carry):
        peer = to_peer(step)
        pl.semaphore_signal(barrier, inc=1, device_id={"sp": peer}, device_id_type=MESH)
        return carry

    lax.fori_loop(1, n_sp, greet, 0)
    pl.semaphore_signal(barrier, inc=1, device_id={"cfg": 1 - core}, device_id_type=MESH)
    for peer in (mirror, mirror_opposite):
        pl.semaphore_signal(
            barrier, inc=1, device_id={"section": 1 - sec, "sp": peer}, device_id_type=MESH
        )

    def transpose_kind(c):
        def body(t, carry):
            rows = pl.ds(pl.multiple_of(t * 16, 16), 16)
            stage[c, :, rows, :] = jnp.swapaxes(xin[c, rows], 0, 1)
            return carry

        lax.fori_loop(0, tok // 16, body, 0)

    def landing(c, source):
        if c == 0:
            return qland.at[source]
        rows = pl.ds(pl.multiple_of(source * tok, tok), tok)
        if c == 1:
            return kland.at[:, rows, :]
        return vaug.at[:, rows, pl.ds(0, hd)]

    def qkv_copy(c, target):
        return pltpu.make_async_remote_copy(
            src_ref=stage.at[c, pl.ds(2 * target, 2)],
            dst_ref=landing(c, me),
            send_sem=s_sem.at[c],
            recv_sem=q_sem.at[me] if c == 0 else r_sem.at[c],
            device_id={"sp": target},
            device_id_type=MESH,
        )

    def query_arrival(source):
        return pltpu.make_async_remote_copy(
            src_ref=qland.at[source],
            dst_ref=qland.at[source],
            send_sem=s_sem.at[0],
            recv_sem=q_sem.at[source],
            device_id={"sp": source},
            device_id_type=MESH,
        )

    def all_sent(held, sem):
        pltpu.make_async_remote_copy(
            src_ref=held, dst_ref=held, send_sem=sem, recv_sem=sem,
            device_id={"cfg": 1 - core}, device_id_type=MESH,
        ).wait_send()

    def all_arrived(held, sem):
        pltpu.make_async_remote_copy(
            src_ref=held, dst_ref=held, send_sem=sem, recv_sem=sem,
            device_id={"cfg": 1 - core}, device_id_type=MESH,
        ).wait_recv()

    def own_copy(c):
        return pltpu.make_async_copy(
            stage.at[c, pl.ds(2 * me, 2)], landing(c, me), own_sem.at[c]
        )

    def send_kind(c):
        def body(step, carry):
            qkv_copy(c, to_peer(n_sp - step)).start()
            return carry

        lax.fori_loop(1, n_sp, body, 0)
        own_copy(c).start()

    loads[1].wait()
    loads[2].start()
    loads[0].start()
    for small in smalls:
        small.start()
    transpose_kind(1)
    loads[2].wait()
    transpose_kind(2)
    pl.semaphore_wait(barrier, n_sp + 2)

    def to_relay(c):
        target = to_peer(across)
        return pltpu.make_async_remote_copy(
            src_ref=stage.at[c, pl.ds(2 * target, 2)],
            dst_ref=relay.at[c - 1],
            send_sem=s_sem.at[c],
            recv_sem=relay_r.at[c - 1],
            device_id={"section": 1, "sp": mirror},
            device_id_type=MESH,
        )

    def onward(c):
        return pltpu.make_async_remote_copy(
            src_ref=relay.at[c - 1],
            dst_ref=landing(c, mirror),
            send_sem=relay_s.at[c - 1],
            recv_sem=r_sem.at[c],
            device_id={"section": 0, "sp": mirror_opposite},
            device_id_type=MESH,
        )

    def relay_in(c):
        return pltpu.make_async_remote_copy(
            src_ref=relay.at[c - 1],
            dst_ref=relay.at[c - 1],
            send_sem=relay_s.at[c - 1],
            recv_sem=relay_r.at[c - 1],
            device_id={"section": 0, "sp": mirror},
            device_id_type=MESH,
        )

    def send_most(c):
        def body(step, carry):
            @pl.when(jnp.logical_or(sec == 1, n_sp - step != across))
            def _():
                qkv_copy(c, to_peer(n_sp - step)).start()

            return carry

        lax.fori_loop(1, n_sp, body, 0)
        own_copy(c).start()

    @pl.when(sec == 0)
    def _():
        for c in RELAYED:
            to_relay(c).start()

    (send_most if 1 in RELAYED else send_kind)(1)

    @pl.when(sec == 1)
    def _():
        for c in RELAYED:
            relay_in(c).wait_recv()
            onward(c).start()

    (send_most if 2 in RELAYED else send_kind)(2)
    loads[0].wait()
    transpose_kind(0)

    def send_query(step, carry):
        qkv_copy(0, to_peer(step)).start()
        return carry

    lax.fori_loop(1, n_sp, send_query, 0)
    own_copy(0).start()

    for small in smalls:
        small.wait()
    count = cnt[0, 0]
    head_id = (2 * me + core).astype(F32)
    dims = lax.broadcasted_iota(jnp.int32, (8, hd), 1).astype(F32)
    freq = jnp.exp(-math.log(10000.0) * dims / hd)
    gate[...] = 1.0 + 0.5 * jnp.sin(ts[0, 0].astype(F32) * freq + 0.7 * head_id)

    key_rows = lax.broadcasted_iota(jnp.int32, (seq, hd), 0)
    ones = jnp.where(key_rows < count, 1.0, 0.0).astype(BF16)
    vaug[0, :, hd:] = ones
    vaug[1, :, hd:] = ones

    for t in range(width // 16):
        stacked = jnp.swapaxes(wi[t * 16:t * 16 + 16], 0, 1).reshape(heads // 2, 2, 16, hd)
        chosen = jnp.where(core == 0, stacked[:, 0], stacked[:, 1])
        for g in range(heads // 2):
            for copy in (0, width):
                w2[copy + t * 16:copy + t * 16 + 16, g * hd:(g + 1) * hd] = chosen[g]

    w2_copy = pltpu.make_async_copy(w2, w2_out, out_sem.at[0])
    w2_copy.start()

    @pl.when(sec == 1)
    def _():
        eye = lax.broadcasted_iota(jnp.int32, (tok, tok), 0) == lax.broadcasted_iota(
            jnp.int32, (tok, tok), 1
        )
        wanted = jnp.sum(
            jnp.where(eye, jnp.broadcast_to(bm[...], (tok, tok)).astype(F32), 0.0),
            axis=1, keepdims=True,
        ).astype(jnp.int32)
        owner = wanted // tok
        row = wanted - owner * tok
        for onehot, (start, size) in zip(onehots, parts):
            depth = size // 2
            inside = row - start
            upper = (inside >= depth).astype(jnp.int32)
            slot = owner * depth + inside - upper * depth
            here = jnp.logical_and(inside >= 0, inside < size)
            places = lax.broadcasted_iota(jnp.int32, (tok, n_sp * depth), 1)
            for side in (0, 1):
                target = jnp.where(jnp.logical_and(here, upper == side), slot, -1)
                onehot[side] = jnp.where(places == target, 1.0, 0.0).astype(BF16)

    others = pl.ds(0, (n_sp - 1) * tok)

    def wait_kind(c):
        all_arrived(
            kland.at[:, others] if c == 1 else vaug.at[:, others, pl.ds(0, hd)], r_sem.at[c]
        )
        own_copy(c).wait()

    quarter = seq // 4
    tail_ok = 3 * quarter + lax.broadcasted_iota(jnp.int32, (quarter, hd), 0) < count
    wait_kind(1)
    for h in (0, 1):
        for part in range(4):
            rows = slice(part * quarter, (part + 1) * quarter)
            block = kland[h, rows].astype(F32)
            if part == 3:
                block = jnp.where(tail_ok, block, kland[h, 0:16].astype(F32)[0:1])
            kt[h, :, rows] = block.T.astype(BF16)
    wait_kind(2)
    for h in (0, 1):
        tail = vaug[h, 3 * quarter:, :hd].astype(F32)
        vaug[h, 3 * quarter:, :hd] = jnp.where(tail_ok, tail, 0.0).astype(BF16)

    def sibling_copy(source):
        return pltpu.make_async_remote_copy(
            src_ref=att_send.at[source],
            dst_ref=att_recv.at[source],
            send_sem=sib_s,
            recv_sem=sib_r.at[source],
            device_id={"cfg": 1 - core},
            device_id_type=MESH,
        )

    def branch_copy(part, target):
        rows = pl.ds(*parts[part])
        return pltpu.make_async_remote_copy(
            src_ref=brs.at[target, rows],
            dst_ref=brl.at[me, rows],
            send_sem=br_s.at[part],
            recv_sem=br_r.at[part],
            device_id={"sp": target},
            device_id_type=MESH,
        )

    def branches(blocks, part):
        return blocks.at[pl.ds(0, n_sp - 1), pl.ds(*parts[part])]

    def attend(step):
        source = query_peer(step)
        for h in (0, 1):
            sc[h] = jnp.dot(qland[source, h], kt[h], preferred_element_type=F32)
        done = []
        for h in (0, 1):
            top = jnp.max(sc[h], axis=1, keepdims=True) * scale
            weights = jnp.exp2(sc[h] * scale - top).astype(BF16)
            mixed = jnp.dot(weights, vaug[h], preferred_element_type=F32)
            done.append(mixed[:, :hd] / mixed[:, hd:])
        att_mine[source] = jnp.where(core == 0, done[0], done[1]).astype(BF16)
        att_send[source] = jnp.where(core == 0, done[1], done[0]).astype(BF16)
        sibling_copy(source).start()

    def combine(step):
        source = query_peer(step)
        sibling_copy(source).wait_recv()
        mine = att_mine[source].astype(F32)
        theirs = att_recv[source].astype(F32)
        cond = jnp.where(core == 0, mine, theirs)
        uncond = jnp.where(core == 0, theirs, mine)
        guided = uncond + 5.0 * (cond - uncond)
        position = source * tok + lax.broadcasted_iota(jnp.int32, (tok, hd), 0)
        return source, jnp.where(position < count, gate[0:1] * guided, 0.0).astype(BF16)

    def keep(step):
        target, block = combine(step)
        brs[target] = block

    def send_part(part, step):
        branch_copy(part, query_peer(step)).start()

    own_copy(0).wait()
    attend(0)

    def first(step, carry):
        query_arrival(query_peer(step)).wait_recv()
        attend(step)

        @pl.when(step == 1)
        def _():
            source, block = combine(0)
            brl[source] = block

        @pl.when(step > 1)
        def _():
            keep(step - 1)

        return carry

    def release(step, carry):
        send_part(0, step)
        return carry

    def later(step, carry):
        query_arrival(query_peer(step)).wait_recv()
        attend(step)
        keep(step - 1)
        send_part(0, step - 1)
        return carry

    hold = n_sp - 1 if n_sp < HOLD else HOLD
    lax.fori_loop(1, hold, first, 0)
    lax.fori_loop(1, hold - 1, release, 0)
    lax.fori_loop(hold, n_sp, later, 0)
    keep(n_sp - 1)
    send_part(0, n_sp - 1)

    for part in range(1, len(parts)):
        def send_rest(step, carry, part=part):
            send_part(part, step)
            return carry

        lax.fori_loop(1, n_sp, send_rest, 0)

    def swap_copy(part):
        rows = pl.ds(parts[part][0] // 2, parts[part][1] // 2)
        return pltpu.make_async_remote_copy(
            src_ref=psum_send.at[rows], dst_ref=psum_recv.at[rows],
            send_sem=ps_s.at[part], recv_sem=ps_r.at[part],
            device_id={"cfg": 1 - core}, device_id_type=MESH,
        )

    def latent_copy(part, target):
        rows = pl.ds(parts[part][0] // 2, parts[part][1] // 2)
        return pltpu.make_async_remote_copy(
            src_ref=lat_mine.at[rows], dst_ref=tables[part].at[me],
            send_sem=lat_s.at[part], recv_sem=lat_r.at[part],
            device_id={"section": 1, "sp": target}, device_id_type=MESH,
        )

    for c in (0, 1, 2):
        all_sent(stage.at[c, pl.ds(0, 2 * (n_sp - 1))], s_sem.at[c])
    all_sent(att_send, sib_s)

    wanted_copy = pltpu.make_async_copy(wanted_held, wanted_out, out_sem.at[1])
    brl_copy = pltpu.make_async_copy(brl, brl_out, out_sem.at[2])

    @pl.when(sec == 0)
    def _():
        for part, (start, size) in enumerate(parts):
            all_arrived(branches(brl, part), br_r.at[part])
            total = jnp.zeros((size, width), F32)
            for source in range(n_sp):
                total = total + lax.dot_general(
                    brl[source, start:start + size], wo[2 * source + core],
                    (((1,), (1,)), ((), ())), preferred_element_type=F32,
                )
            packed = jnp.concatenate([total[:size // 2], total[size // 2:]], axis=1)
            rows = slice(start // 2, (start + size) // 2)
            psum_send[rows] = packed
            swap_copy(part).start()
            swap_copy(part).wait_recv()
            lat_mine[rows] = (packed + psum_recv[rows]).astype(BF16)

            def hand(step, carry, part=part):
                latent_copy(part, to_peer(step)).start()
                return carry

            lax.fori_loop(0, n_sp, hand, 0)

        wanted_held[...] = jnp.zeros_like(wanted_held)
        wanted_copy.start()
        brl_copy.start()
        for part in range(len(parts)):
            all_sent(branches(brs, part), br_s.at[part])
            all_sent(tables[part], lat_s.at[part])
            swap_copy(part).wait_send()

    @pl.when(sec == 1)
    def _():
        lanes = lax.broadcasted_iota(jnp.int32, (tok, 2 * width), 1)

        for part in range(len(parts)):
            all_arrived(branches(brl, part), br_r.at[part])
        brl_copy.start()
        for part in range(len(parts)):
            all_sent(branches(brs, part), br_s.at[part])
        picked = jnp.zeros((tok, 2 * width), F32)
        for part, (onehot, table) in enumerate(zip(onehots, tables)):
            all_arrived(table, lat_r.at[part])
            rows = table[...].reshape(n_sp * parts[part][1] // 2, 2 * width)
            low = jnp.dot(onehot[0], rows, preferred_element_type=F32)
            high = jnp.dot(onehot[1], rows, preferred_element_type=F32)
            picked = picked + jnp.where(lanes < width, low, high)
        wanted_held[...] = picked.astype(BF16)
        wanted_copy.start()

    w2_copy.wait()
    brl_copy.wait()
    wanted_copy.wait()

    @pl.when(sec == 1)
    def _():
        for c in RELAYED:
            onward(c).wait_send()


def lift_kernel(wanted_ref, w2_ref, brl_ref, out_ref):
    groups, _, hd = brl_ref.shape
    raised = jnp.dot(wanted_ref[...], w2_ref[...], preferred_element_type=F32)
    result = jnp.stack(
        [
            (brl_ref[g].astype(F32) + raised[:, g * hd:(g + 1) * hd]).astype(BF16)
            for g in range(groups)
        ]
    )
    out_ref[...] = jnp.swapaxes(result, 0, 1)


def on_device(qkv, counts, timesteps, block_map, w_out, w_in):
    n_sp = lax.axis_size("sp")
    tok, _, heads, hd = qkv.shape[2:]
    width = w_out.shape[2]
    seq = tok * n_sp
    half = tok // 2
    halves = [size // 2 for _, size in part_rows(tok)]
    dma = pltpu.SemaphoreType.DMA
    hbm = pl.BlockSpec(memory_space=pltpu.HBM)

    def body(*refs):
        kernel(n_sp, tok, heads, hd, width, *refs)

    brl, wanted, w2 = pl.pallas_call(
        body,
        name="guided_attention",
        out_shape=(
            jax.ShapeDtypeStruct((n_sp, tok, hd), BF16),
            jax.ShapeDtypeStruct((tok, 2 * width), BF16),
            jax.ShapeDtypeStruct((2 * width, heads // 2 * hd), BF16),
        ),
        in_specs=[hbm] * 6,
        out_specs=(hbm, hbm, hbm),
        scratch_shapes=[
            pltpu.VMEM((3, tok, heads, hd), BF16),
            pltpu.VMEM((3, heads, tok, hd), BF16),
            pltpu.VMEM((n_sp, 2, tok, hd), BF16),
            pltpu.VMEM((2, seq, hd), BF16),
            pltpu.VMEM((2, seq, 2 * hd), BF16),
            pltpu.VMEM((2, hd, seq), BF16),
            pltpu.VMEM((2, tok, seq), F32),
            pltpu.VMEM((n_sp, tok, hd), BF16),
            pltpu.VMEM((n_sp, tok, hd), BF16),
            pltpu.VMEM((n_sp, tok, hd), BF16),
            pltpu.VMEM((n_sp, tok, hd), BF16),
            pltpu.VMEM((n_sp, tok, hd), BF16),
            pltpu.VMEM((2, 2, tok, hd), BF16),
            pltpu.VMEM((half, 2 * width), BF16),
            *[pltpu.VMEM((n_sp, depth, 2 * width), BF16) for depth in halves],
            pltpu.VMEM((half, 2 * width), F32),
            pltpu.VMEM((half, 2 * width), F32),
            *[pltpu.VMEM((2, tok, n_sp * depth), BF16) for depth in halves],
            pltpu.VMEM((heads, width, hd), BF16),
            pltpu.VMEM((width, heads, hd), BF16),
            pltpu.VMEM((8, hd), F32),
            pltpu.VMEM((tok, 2 * width), BF16),
            pltpu.VMEM((2 * width, heads // 2 * hd), BF16),
            pltpu.SMEM((1, 1), jnp.int32),
            pltpu.SMEM((1, 1), jnp.int32),
            pltpu.VMEM((1, tok), jnp.int32),
            dma((3,)), dma((5,)), dma((3,)),
            dma((3,)), dma((3,)), dma((n_sp,)),
            dma, dma((n_sp,)),
            dma((3,)), dma((3,)),
            dma((3,)), dma((3,)),
            dma((3,)), dma((3,)),
            dma((2,)), dma((2,)), dma((3,)),
        ],
        compiler_params=pltpu.CompilerParams(
            collective_id=0, has_side_effects=True, vmem_limit_bytes=56 << 20
        ),
    )(
        qkv[0, 0],
        counts,
        timesteps,
        block_map.reshape(1, tok),
        jnp.swapaxes(w_out, 1, 2),
        w_in,
    )
    result = pl.pallas_call(
        lift_kernel,
        name="lift",
        out_shape=jax.ShapeDtypeStruct((tok, heads // 2, hd), BF16),
    )(wanted, w2, brl)
    return result[None, :, None]


def solution(mesh):
    placed = (
        P("section", "cfg", ("req", "sp"), None, None, None),
        P("section", "req"),
        P("section", "req"),
        P(("req", "sp")),
        P(),
        P(),
    )
    return jax.shard_map(
        on_device,
        mesh=mesh,
        in_specs=placed,
        out_specs=P("section", ("req", "sp"), "cfg", None, None),
        check_vma=False,
    )
```

```python
import math

import jax
import jax.numpy as jnp
from jax import lax
from jax.experimental import pallas as pl
from jax.experimental.pallas import tpu as pltpu
from jax.sharding import PartitionSpec as P

MESH = pl.DeviceIdType.MESH
F32 = jnp.float32
BF16 = jnp.bfloat16
HOLD = 12
RELAYED = (1,)


def part_rows(tok):
    steps = tok // 32
    sizes = (32 * (steps * 3 // 5), 32 * (steps - 1 - steps * 3 // 5), 32)
    return tuple((sum(sizes[:n]), size) for n, size in enumerate(sizes))


def kernel(
    n_sp, tok, heads, hd, width,
    qkv_ref, cnt_ref, ts_ref, bm_ref, wo_ref, wi_ref, brl_out, wanted_out, w2_out,
    xin, stage, qland, kland, vaug, kt, sc, att_mine, att_send, att_recv, brs, brl, relay,
    lat_mine, lat_a, lat_b, lat_c, psum_send, psum_recv, onehot_a, onehot_b, onehot_c, wo, wi, gate,
    wanted_held, w2,
    cnt, ts, bm,
    in_sem, w_sem, own_sem, s_sem, r_sem, q_sem, sib_s, sib_r, br_s, br_r, ps_s, ps_r, lat_s, lat_r,
    relay_s, relay_r, out_sem,
):
    seq = tok * n_sp
    parts = part_rows(tok)
    tables = (lat_a, lat_b, lat_c)
    onehots = (onehot_a, onehot_b, onehot_c)
    n_z = n_sp // 2
    sec = lax.axis_index("section")
    core = lax.axis_index("cfg")
    me = lax.axis_index("sp")
    scale = hd ** -0.5 * math.log2(math.e)

    def offset(step):
        turn = step // 2
        dz = ((turn + 1) // 2) * (1 - 2 * ((turn + 1) % 2))
        return step % 2, dz

    def to_peer(step):
        dx, dz = offset(step)
        return ((me // n_z + dx) % 2) * n_z + (me % n_z + dz + n_z) % n_z

    def query_peer(step):
        return from_peer(step)

    def from_peer(step):
        dx, dz = offset(step)
        return ((me // n_z + dx) % 2) * n_z + (me % n_z - dz + n_z) % n_z

    across = n_sp - 2
    mirror = (1 - me // n_z) * n_z + me % n_z
    mirror_opposite = (1 - me // n_z) * n_z + (me % n_z + n_z // 2) % n_z

    loads = [
        pltpu.make_async_copy(qkv_ref.at[:, c], xin.at[c], in_sem.at[c]) for c in (0, 1, 2)
    ]
    loads[1].start()
    smalls = [
        pltpu.make_async_copy(source, held, w_sem.at[n])
        for n, (source, held) in enumerate(
            ((wo_ref, wo), (wi_ref, wi), (cnt_ref, cnt), (ts_ref, ts), (bm_ref, bm))
        )
    ]

    barrier = pltpu.get_barrier_semaphore()

    def greet(step, carry):
        peer = to_peer(step)
        pl.semaphore_signal(barrier, inc=1, device_id={"sp": peer}, device_id_type=MESH)
        return carry

    lax.fori_loop(1, n_sp, greet, 0)
    pl.semaphore_signal(barrier, inc=1, device_id={"cfg": 1 - core}, device_id_type=MESH)
    for peer in (mirror, mirror_opposite):
        pl.semaphore_signal(
            barrier, inc=1, device_id={"section": 1 - sec, "sp": peer}, device_id_type=MESH
        )

    def transpose_kind(c):
        def body(t, carry):
            rows = pl.ds(pl.multiple_of(t * 16, 16), 16)
            stage[c, :, rows, :] = jnp.swapaxes(xin[c, rows], 0, 1)
            return carry

        lax.fori_loop(0, tok // 16, body, 0)

    def landing(c, source):
        if c == 0:
            return qland.at[source]
        rows = pl.ds(pl.multiple_of(source * tok, tok), tok)
        if c == 1:
            return kland.at[:, rows, :]
        return vaug.at[:, rows, pl.ds(0, hd)]

    def qkv_copy(c, target):
        return pltpu.make_async_remote_copy(
            src_ref=stage.at[c, pl.ds(2 * target, 2)],
            dst_ref=landing(c, me),
            send_sem=s_sem.at[c],
            recv_sem=q_sem.at[me] if c == 0 else r_sem.at[c],
            device_id={"sp": target},
            device_id_type=MESH,
        )

    def query_arrival(source):
        return pltpu.make_async_remote_copy(
            src_ref=qland.at[source],
            dst_ref=qland.at[source],
            send_sem=s_sem.at[0],
            recv_sem=q_sem.at[source],
            device_id={"sp": source},
            device_id_type=MESH,
        )

    def all_sent(held, sem):
        pltpu.make_async_remote_copy(
            src_ref=held, dst_ref=held, send_sem=sem, recv_sem=sem,
            device_id={"cfg": 1 - core}, device_id_type=MESH,
        ).wait_send()

    def all_arrived(held, sem):
        pltpu.make_async_remote_copy(
            src_ref=held, dst_ref=held, send_sem=sem, recv_sem=sem,
            device_id={"cfg": 1 - core}, device_id_type=MESH,
        ).wait_recv()

    def own_copy(c):
        return pltpu.make_async_copy(
            stage.at[c, pl.ds(2 * me, 2)], landing(c, me), own_sem.at[c]
        )

    def send_kind(c):
        def body(step, carry):
            qkv_copy(c, to_peer(n_sp - step)).start()
            return carry

        lax.fori_loop(1, n_sp, body, 0)
        own_copy(c).start()

    loads[1].wait()
    loads[2].start()
    loads[0].start()
    for small in smalls:
        small.start()
    transpose_kind(1)
    loads[2].wait()
    transpose_kind(2)
    pl.semaphore_wait(barrier, n_sp + 2)

    def to_relay(c):
        target = to_peer(across)
        return pltpu.make_async_remote_copy(
            src_ref=stage.at[c, pl.ds(2 * target, 2)],
            dst_ref=relay.at[c - 1],
            send_sem=s_sem.at[c],
            recv_sem=relay_r.at[c - 1],
            device_id={"section": 1, "sp": mirror},
            device_id_type=MESH,
        )

    def onward(c):
        return pltpu.make_async_remote_copy(
            src_ref=relay.at[c - 1],
            dst_ref=landing(c, mirror),
            send_sem=relay_s.at[c - 1],
            recv_sem=r_sem.at[c],
            device_id={"section": 0, "sp": mirror_opposite},
            device_id_type=MESH,
        )

    def relay_in(c):
        return pltpu.make_async_remote_copy(
            src_ref=relay.at[c - 1],
            dst_ref=relay.at[c - 1],
            send_sem=relay_s.at[c - 1],
            recv_sem=relay_r.at[c - 1],
            device_id={"section": 0, "sp": mirror},
            device_id_type=MESH,
        )

    def send_most(c):
        def body(step, carry):
            @pl.when(jnp.logical_or(sec == 1, n_sp - step != across))
            def _():
                qkv_copy(c, to_peer(n_sp - step)).start()

            return carry

        lax.fori_loop(1, n_sp, body, 0)
        own_copy(c).start()

    @pl.when(sec == 0)
    def _():
        for c in RELAYED:
            to_relay(c).start()

    (send_most if 1 in RELAYED else send_kind)(1)

    @pl.when(sec == 1)
    def _():
        for c in RELAYED:
            relay_in(c).wait_recv()
            onward(c).start()

    (send_most if 2 in RELAYED else send_kind)(2)
    loads[0].wait()
    transpose_kind(0)

    def send_query(step, carry):
        qkv_copy(0, to_peer(step)).start()
        return carry

    lax.fori_loop(1, n_sp, send_query, 0)
    own_copy(0).start()

    for small in smalls:
        small.wait()
    count = cnt[0, 0]
    head_id = (2 * me + core).astype(F32)
    dims = lax.broadcasted_iota(jnp.int32, (8, hd), 1).astype(F32)
    freq = jnp.exp(-math.log(10000.0) * dims / hd)
    gate[...] = 1.0 + 0.5 * jnp.sin(ts[0, 0].astype(F32) * freq + 0.7 * head_id)

    key_rows = lax.broadcasted_iota(jnp.int32, (seq, hd), 0)
    ones = jnp.where(key_rows < count, 1.0, 0.0).astype(BF16)
    vaug[0, :, hd:] = ones
    vaug[1, :, hd:] = ones

    for t in range(width // 16):
        stacked = jnp.swapaxes(wi[t * 16:t * 16 + 16], 0, 1).reshape(heads // 2, 2, 16, hd)
        chosen = jnp.where(core == 0, stacked[:, 0], stacked[:, 1])
        for g in range(heads // 2):
            for copy in (0, width):
                w2[copy + t * 16:copy + t * 16 + 16, g * hd:(g + 1) * hd] = chosen[g]

    w2_copy = pltpu.make_async_copy(w2, w2_out, out_sem.at[0])
    w2_copy.start()

    @pl.when(sec == 1)
    def _():
        eye = lax.broadcasted_iota(jnp.int32, (tok, tok), 0) == lax.broadcasted_iota(
            jnp.int32, (tok, tok), 1
        )
        wanted = jnp.sum(
            jnp.where(eye, jnp.broadcast_to(bm[...], (tok, tok)).astype(F32), 0.0),
            axis=1, keepdims=True,
        ).astype(jnp.int32)
        owner = wanted // tok
        row = wanted - owner * tok
        for onehot, (start, size) in zip(onehots, parts):
            depth = size // 2
            inside = row - start
            upper = (inside >= depth).astype(jnp.int32)
            slot = owner * depth + inside - upper * depth
            here = jnp.logical_and(inside >= 0, inside < size)
            places = lax.broadcasted_iota(jnp.int32, (tok, n_sp * depth), 1)
            for side in (0, 1):
                target = jnp.where(jnp.logical_and(here, upper == side), slot, -1)
                onehot[side] = jnp.where(places == target, 1.0, 0.0).astype(BF16)

    others = pl.ds(0, (n_sp - 1) * tok)

    def wait_kind(c):
        all_arrived(
            kland.at[:, others] if c == 1 else vaug.at[:, others, pl.ds(0, hd)], r_sem.at[c]
        )
        own_copy(c).wait()

    quarter = seq // 4
    tail_ok = 3 * quarter + lax.broadcasted_iota(jnp.int32, (quarter, hd), 0) < count
    wait_kind(1)
    for h in (0, 1):
        for part in range(4):
            rows = slice(part * quarter, (part + 1) * quarter)
            block = kland[h, rows].astype(F32)
            if part == 3:
                block = jnp.where(tail_ok, block, kland[h, 0:16].astype(F32)[0:1])
            kt[h, :, rows] = block.T.astype(BF16)
    wait_kind(2)
    for h in (0, 1):
        tail = vaug[h, 3 * quarter:, :hd].astype(F32)
        vaug[h, 3 * quarter:, :hd] = jnp.where(tail_ok, tail, 0.0).astype(BF16)

    def sibling_copy(source):
        return pltpu.make_async_remote_copy(
            src_ref=att_send.at[source],
            dst_ref=att_recv.at[source],
            send_sem=sib_s,
            recv_sem=sib_r.at[source],
            device_id={"cfg": 1 - core},
            device_id_type=MESH,
        )

    def branch_copy(part, target):
        rows = pl.ds(*parts[part])
        return pltpu.make_async_remote_copy(
            src_ref=brs.at[target, rows],
            dst_ref=brl.at[me, rows],
            send_sem=br_s.at[part],
            recv_sem=br_r.at[part],
            device_id={"sp": target},
            device_id_type=MESH,
        )

    def branches(blocks, part):
        return blocks.at[pl.ds(0, n_sp - 1), pl.ds(*parts[part])]

    def attend(step):
        source = query_peer(step)
        for h in (0, 1):
            sc[h] = jnp.dot(qland[source, h], kt[h], preferred_element_type=F32)
        done = []
        for h in (0, 1):
            top = jnp.max(sc[h], axis=1, keepdims=True) * scale
            weights = jnp.exp2(sc[h] * scale - top).astype(BF16)
            mixed = jnp.dot(weights, vaug[h], preferred_element_type=F32)
            done.append(mixed[:, :hd] / mixed[:, hd:])
        att_mine[source] = jnp.where(core == 0, done[0], done[1]).astype(BF16)
        att_send[source] = jnp.where(core == 0, done[1], done[0]).astype(BF16)
        sibling_copy(source).start()

    def combine(step):
        source = query_peer(step)
        sibling_copy(source).wait_recv()
        mine = att_mine[source].astype(F32)
        theirs = att_recv[source].astype(F32)
        cond = jnp.where(core == 0, mine, theirs)
        uncond = jnp.where(core == 0, theirs, mine)
        guided = uncond + 5.0 * (cond - uncond)
        position = source * tok + lax.broadcasted_iota(jnp.int32, (tok, hd), 0)
        return source, jnp.where(position < count, gate[0:1] * guided, 0.0).astype(BF16)

    def keep(step):
        target, block = combine(step)
        brs[target] = block

    def send_part(part, step):
        branch_copy(part, query_peer(step)).start()

    own_copy(0).wait()
    attend(0)

    def first(step, carry):
        query_arrival(query_peer(step)).wait_recv()
        attend(step)

        @pl.when(step == 1)
        def _():
            source, block = combine(0)
            brl[source] = block

        @pl.when(step > 1)
        def _():
            keep(step - 1)

        return carry

    def release(step, carry):
        send_part(0, step)
        return carry

    def later(step, carry):
        query_arrival(query_peer(step)).wait_recv()
        attend(step)
        keep(step - 1)
        send_part(0, step - 1)
        return carry

    hold = n_sp - 1 if n_sp < HOLD else HOLD
    lax.fori_loop(1, hold, first, 0)
    lax.fori_loop(1, hold - 1, release, 0)
    lax.fori_loop(hold, n_sp, later, 0)
    keep(n_sp - 1)
    send_part(0, n_sp - 1)

    for part in range(1, len(parts)):
        def send_rest(step, carry, part=part):
            send_part(part, step)
            return carry

        lax.fori_loop(1, n_sp, send_rest, 0)

    def swap_copy(part):
        rows = pl.ds(parts[part][0] // 2, parts[part][1] // 2)
        return pltpu.make_async_remote_copy(
            src_ref=psum_send.at[rows], dst_ref=psum_recv.at[rows],
            send_sem=ps_s.at[part], recv_sem=ps_r.at[part],
            device_id={"cfg": 1 - core}, device_id_type=MESH,
        )

    def latent_copy(part, target):
        rows = pl.ds(parts[part][0] // 2, parts[part][1] // 2)
        return pltpu.make_async_remote_copy(
            src_ref=lat_mine.at[rows], dst_ref=tables[part].at[me],
            send_sem=lat_s.at[part], recv_sem=lat_r.at[part],
            device_id={"section": 1, "sp": target}, device_id_type=MESH,
        )

    for c in (0, 1, 2):
        all_sent(stage.at[c, pl.ds(0, 2 * (n_sp - 1))], s_sem.at[c])
    all_sent(att_send, sib_s)

    wanted_copy = pltpu.make_async_copy(wanted_held, wanted_out, out_sem.at[1])
    brl_copy = pltpu.make_async_copy(brl, brl_out, out_sem.at[2])

    @pl.when(sec == 0)
    def _():
        for part, (start, size) in enumerate(parts):
            all_arrived(branches(brl, part), br_r.at[part])
            total = jnp.zeros((size, width), F32)
            for source in range(n_sp):
                total = total + lax.dot_general(
                    brl[source, start:start + size], wo[2 * source + core],
                    (((1,), (1,)), ((), ())), preferred_element_type=F32,
                )
            packed = jnp.concatenate([total[:size // 2], total[size // 2:]], axis=1)
            rows = slice(start // 2, (start + size) // 2)
            psum_send[rows] = packed
            swap_copy(part).start()
            swap_copy(part).wait_recv()
            lat_mine[rows] = (packed + psum_recv[rows]).astype(BF16)

            def hand(step, carry, part=part):
                latent_copy(part, to_peer(n_sp - 1 - step)).start()
                return carry

            lax.fori_loop(0, n_sp, hand, 0)

        wanted_held[...] = jnp.zeros_like(wanted_held)
        wanted_copy.start()
        brl_copy.start()
        for part in range(len(parts)):
            all_sent(branches(brs, part), br_s.at[part])
            all_sent(tables[part], lat_s.at[part])
            swap_copy(part).wait_send()

    @pl.when(sec == 1)
    def _():
        lanes = lax.broadcasted_iota(jnp.int32, (tok, 2 * width), 1)

        for part in range(len(parts)):
            all_arrived(branches(brl, part), br_r.at[part])
        brl_copy.start()
        for part in range(len(parts)):
            all_sent(branches(brs, part), br_s.at[part])
        picked = jnp.zeros((tok, 2 * width), F32)
        for part, (onehot, table) in enumerate(zip(onehots, tables)):
            all_arrived(table, lat_r.at[part])
            rows = table[...].reshape(n_sp * parts[part][1] // 2, 2 * width)
            low = jnp.dot(onehot[0], rows, preferred_element_type=F32)
            high = jnp.dot(onehot[1], rows, preferred_element_type=F32)
            picked = picked + jnp.where(lanes < width, low, high)
        wanted_held[...] = picked.astype(BF16)
        wanted_copy.start()

    w2_copy.wait()
    brl_copy.wait()
    wanted_copy.wait()

    @pl.when(sec == 1)
    def _():
        for c in RELAYED:
            onward(c).wait_send()


def lift_kernel(wanted_ref, w2_ref, brl_ref, out_ref):
    groups, _, hd = brl_ref.shape
    raised = jnp.dot(wanted_ref[...], w2_ref[...], preferred_element_type=F32)
    result = jnp.stack(
        [
            (brl_ref[g].astype(F32) + raised[:, g * hd:(g + 1) * hd]).astype(BF16)
            for g in range(groups)
        ]
    )
    out_ref[...] = jnp.swapaxes(result, 0, 1)


def on_device(qkv, counts, timesteps, block_map, w_out, w_in):
    n_sp = lax.axis_size("sp")
    tok, _, heads, hd = qkv.shape[2:]
    width = w_out.shape[2]
    seq = tok * n_sp
    half = tok // 2
    halves = [size // 2 for _, size in part_rows(tok)]
    dma = pltpu.SemaphoreType.DMA
    hbm = pl.BlockSpec(memory_space=pltpu.HBM)

    def body(*refs):
        kernel(n_sp, tok, heads, hd, width, *refs)

    brl, wanted, w2 = pl.pallas_call(
        body,
        name="guided_attention",
        out_shape=(
            jax.ShapeDtypeStruct((n_sp, tok, hd), BF16),
            jax.ShapeDtypeStruct((tok, 2 * width), BF16),
            jax.ShapeDtypeStruct((2 * width, heads // 2 * hd), BF16),
        ),
        in_specs=[hbm] * 6,
        out_specs=(hbm, hbm, hbm),
        scratch_shapes=[
            pltpu.VMEM((3, tok, heads, hd), BF16),
            pltpu.VMEM((3, heads, tok, hd), BF16),
            pltpu.VMEM((n_sp, 2, tok, hd), BF16),
            pltpu.VMEM((2, seq, hd), BF16),
            pltpu.VMEM((2, seq, 2 * hd), BF16),
            pltpu.VMEM((2, hd, seq), BF16),
            pltpu.VMEM((2, tok, seq), F32),
            pltpu.VMEM((n_sp, tok, hd), BF16),
            pltpu.VMEM((n_sp, tok, hd), BF16),
            pltpu.VMEM((n_sp, tok, hd), BF16),
            pltpu.VMEM((n_sp, tok, hd), BF16),
            pltpu.VMEM((n_sp, tok, hd), BF16),
            pltpu.VMEM((2, 2, tok, hd), BF16),
            pltpu.VMEM((half, 2 * width), BF16),
            *[pltpu.VMEM((n_sp, depth, 2 * width), BF16) for depth in halves],
            pltpu.VMEM((half, 2 * width), F32),
            pltpu.VMEM((half, 2 * width), F32),
            *[pltpu.VMEM((2, tok, n_sp * depth), BF16) for depth in halves],
            pltpu.VMEM((heads, width, hd), BF16),
            pltpu.VMEM((width, heads, hd), BF16),
            pltpu.VMEM((8, hd), F32),
            pltpu.VMEM((tok, 2 * width), BF16),
            pltpu.VMEM((2 * width, heads // 2 * hd), BF16),
            pltpu.SMEM((1, 1), jnp.int32),
            pltpu.SMEM((1, 1), jnp.int32),
            pltpu.VMEM((1, tok), jnp.int32),
            dma((3,)), dma((5,)), dma((3,)),
            dma((3,)), dma((3,)), dma((n_sp,)),
            dma, dma((n_sp,)),
            dma((3,)), dma((3,)),
            dma((3,)), dma((3,)),
            dma((3,)), dma((3,)),
            dma((2,)), dma((2,)), dma((3,)),
        ],
        compiler_params=pltpu.CompilerParams(
            collective_id=0, has_side_effects=True, vmem_limit_bytes=56 << 20
        ),
    )(
        qkv[0, 0],
        counts,
        timesteps,
        block_map.reshape(1, tok),
        jnp.swapaxes(w_out, 1, 2),
        w_in,
    )
    result = pl.pallas_call(
        lift_kernel,
        name="lift",
        out_shape=jax.ShapeDtypeStruct((tok, heads // 2, hd), BF16),
    )(wanted, w2, brl)
    return result[None, :, None]


def solution(mesh):
    placed = (
        P("section", "cfg", ("req", "sp"), None, None, None),
        P("section", "req"),
        P("section", "req"),
        P(("req", "sp")),
        P(),
        P(),
    )
    return jax.shard_map(
        on_device,
        mesh=mesh,
        in_specs=placed,
        out_specs=P("section", ("req", "sp"), "cfg", None, None),
        check_vma=False,
    )
```

```python
import math

import jax
import jax.numpy as jnp
from jax import lax
from jax.experimental import pallas as pl
from jax.experimental.pallas import tpu as pltpu
from jax.sharding import PartitionSpec as P

MESH = pl.DeviceIdType.MESH
F32 = jnp.float32
BF16 = jnp.bfloat16
HOLD = 12
RELAYED = (1,)


def part_rows(tok):
    steps = tok // 32
    sizes = (32 * (steps * 3 // 5), 32 * (steps - 1 - steps * 3 // 5), 32)
    return tuple((sum(sizes[:n]), size) for n, size in enumerate(sizes))


def kernel(
    n_sp, tok, heads, hd, width,
    qkv_ref, cnt_ref, ts_ref, bm_ref, wo_ref, wi_ref, brl_out, wanted_out, w2_out,
    xin, stage, qland, kland, vaug, kt, sc, att_mine, att_send, att_recv, brs, brl, relay,
    lat_mine, lat_a, lat_b, lat_c, psum_send, psum_recv, onehot_a, onehot_b, onehot_c, wo, wi, gate,
    wanted_held, w2,
    cnt, ts, bm,
    in_sem, w_sem, own_sem, s_sem, r_sem, q_sem, sib_s, sib_r, br_s, br_r, ps_s, ps_r, lat_s, lat_r,
    relay_s, relay_r, out_sem,
):
    seq = tok * n_sp
    parts = part_rows(tok)
    tables = (lat_a, lat_b, lat_c)
    onehots = (onehot_a, onehot_b, onehot_c)
    n_z = n_sp // 2
    sec = lax.axis_index("section")
    core = lax.axis_index("cfg")
    me = lax.axis_index("sp")
    scale = hd ** -0.5 * math.log2(math.e)

    def offset(step):
        turn = step // 2
        dz = ((turn + 1) // 2) * (1 - 2 * ((turn + 1) % 2))
        return step % 2, dz

    def to_peer(step):
        dx, dz = offset(step)
        return ((me // n_z + dx) % 2) * n_z + (me % n_z + dz + n_z) % n_z

    def query_peer(step):
        return from_peer(step)

    def from_peer(step):
        dx, dz = offset(step)
        return ((me // n_z + dx) % 2) * n_z + (me % n_z - dz + n_z) % n_z

    across = n_sp - 2
    mirror = (1 - me // n_z) * n_z + me % n_z
    mirror_opposite = (1 - me // n_z) * n_z + (me % n_z + n_z // 2) % n_z

    loads = [
        pltpu.make_async_copy(qkv_ref.at[:, c], xin.at[c], in_sem.at[c]) for c in (0, 1, 2)
    ]
    loads[1].start()
    smalls = [
        pltpu.make_async_copy(source, held, w_sem.at[n])
        for n, (source, held) in enumerate(
            ((wo_ref, wo), (wi_ref, wi), (cnt_ref, cnt), (ts_ref, ts), (bm_ref, bm))
        )
    ]

    barrier = pltpu.get_barrier_semaphore()

    def greet(step, carry):
        peer = to_peer(step)
        pl.semaphore_signal(barrier, inc=1, device_id={"sp": peer}, device_id_type=MESH)
        return carry

    lax.fori_loop(1, n_sp, greet, 0)
    pl.semaphore_signal(barrier, inc=1, device_id={"cfg": 1 - core}, device_id_type=MESH)
    for peer in (mirror, mirror_opposite):
        pl.semaphore_signal(
            barrier, inc=1, device_id={"section": 1 - sec, "sp": peer}, device_id_type=MESH
        )

    def transpose_kind(c):
        def body(t, carry):
            rows = pl.ds(pl.multiple_of(t * 16, 16), 16)
            stage[c, :, rows, :] = jnp.swapaxes(xin[c, rows], 0, 1)
            return carry

        lax.fori_loop(0, tok // 16, body, 0)

    def landing(c, source):
        if c == 0:
            return qland.at[source]
        rows = pl.ds(pl.multiple_of(source * tok, tok), tok)
        if c == 1:
            return kland.at[:, rows, :]
        return vaug.at[:, rows, pl.ds(0, hd)]

    def qkv_copy(c, target):
        return pltpu.make_async_remote_copy(
            src_ref=stage.at[c, pl.ds(2 * target, 2)],
            dst_ref=landing(c, me),
            send_sem=s_sem.at[c],
            recv_sem=q_sem.at[me] if c == 0 else r_sem.at[c],
            device_id={"sp": target},
            device_id_type=MESH,
        )

    def query_arrival(source):
        return pltpu.make_async_remote_copy(
            src_ref=qland.at[source],
            dst_ref=qland.at[source],
            send_sem=s_sem.at[0],
            recv_sem=q_sem.at[source],
            device_id={"sp": source},
            device_id_type=MESH,
        )

    def all_sent(held, sem):
        pltpu.make_async_remote_copy(
            src_ref=held, dst_ref=held, send_sem=sem, recv_sem=sem,
            device_id={"cfg": 1 - core}, device_id_type=MESH,
        ).wait_send()

    def all_arrived(held, sem):
        pltpu.make_async_remote_copy(
            src_ref=held, dst_ref=held, send_sem=sem, recv_sem=sem,
            device_id={"cfg": 1 - core}, device_id_type=MESH,
        ).wait_recv()

    def own_copy(c):
        return pltpu.make_async_copy(
            stage.at[c, pl.ds(2 * me, 2)], landing(c, me), own_sem.at[c]
        )

    def send_kind(c):
        def body(step, carry):
            qkv_copy(c, to_peer(n_sp - step)).start()
            return carry

        lax.fori_loop(1, n_sp, body, 0)
        own_copy(c).start()

    loads[1].wait()
    loads[2].start()
    loads[0].start()
    for small in smalls:
        small.start()
    transpose_kind(1)
    loads[2].wait()
    transpose_kind(2)
    pl.semaphore_wait(barrier, n_sp + 2)

    def to_relay(c):
        target = to_peer(across)
        return pltpu.make_async_remote_copy(
            src_ref=stage.at[c, pl.ds(2 * target, 2)],
            dst_ref=relay.at[c - 1],
            send_sem=s_sem.at[c],
            recv_sem=relay_r.at[c - 1],
            device_id={"section": 1, "sp": mirror},
            device_id_type=MESH,
        )

    def onward(c):
        return pltpu.make_async_remote_copy(
            src_ref=relay.at[c - 1],
            dst_ref=landing(c, mirror),
            send_sem=relay_s.at[c - 1],
            recv_sem=r_sem.at[c],
            device_id={"section": 0, "sp": mirror_opposite},
            device_id_type=MESH,
        )

    def relay_in(c):
        return pltpu.make_async_remote_copy(
            src_ref=relay.at[c - 1],
            dst_ref=relay.at[c - 1],
            send_sem=relay_s.at[c - 1],
            recv_sem=relay_r.at[c - 1],
            device_id={"section": 0, "sp": mirror},
            device_id_type=MESH,
        )

    def send_most(c):
        def body(step, carry):
            @pl.when(jnp.logical_or(sec == 1, n_sp - step != across))
            def _():
                qkv_copy(c, to_peer(n_sp - step)).start()

            return carry

        lax.fori_loop(1, n_sp, body, 0)
        own_copy(c).start()

    @pl.when(sec == 0)
    def _():
        for c in RELAYED:
            to_relay(c).start()

    (send_most if 1 in RELAYED else send_kind)(1)

    @pl.when(sec == 1)
    def _():
        for c in RELAYED:
            relay_in(c).wait_recv()
            onward(c).start()

    (send_most if 2 in RELAYED else send_kind)(2)
    loads[0].wait()
    transpose_kind(0)

    def send_query(step, carry):
        qkv_copy(0, to_peer(step)).start()
        return carry

    lax.fori_loop(1, n_sp, send_query, 0)
    own_copy(0).start()

    for small in smalls:
        small.wait()
    count = cnt[0, 0]
    head_id = (2 * me + core).astype(F32)
    dims = lax.broadcasted_iota(jnp.int32, (8, hd), 1).astype(F32)
    freq = jnp.exp(-math.log(10000.0) * dims / hd)
    gate[...] = 1.0 + 0.5 * jnp.sin(ts[0, 0].astype(F32) * freq + 0.7 * head_id)

    key_rows = lax.broadcasted_iota(jnp.int32, (seq, hd), 0)
    ones = jnp.where(key_rows < count, 1.0, 0.0).astype(BF16)
    vaug[0, :, hd:] = ones
    vaug[1, :, hd:] = ones

    for t in range(width // 16):
        stacked = jnp.swapaxes(wi[t * 16:t * 16 + 16], 0, 1).reshape(heads // 2, 2, 16, hd)
        chosen = jnp.where(core == 0, stacked[:, 0], stacked[:, 1])
        for g in range(heads // 2):
            for copy in (0, width):
                w2[copy + t * 16:copy + t * 16 + 16, g * hd:(g + 1) * hd] = chosen[g]

    w2_copy = pltpu.make_async_copy(w2, w2_out, out_sem.at[0])
    w2_copy.start()

    @pl.when(sec == 1)
    def _():
        eye = lax.broadcasted_iota(jnp.int32, (tok, tok), 0) == lax.broadcasted_iota(
            jnp.int32, (tok, tok), 1
        )
        wanted = jnp.sum(
            jnp.where(eye, jnp.broadcast_to(bm[...], (tok, tok)).astype(F32), 0.0),
            axis=1, keepdims=True,
        ).astype(jnp.int32)
        owner = wanted // tok
        row = wanted - owner * tok
        for onehot, (start, size) in zip(onehots, parts):
            depth = size // 2
            inside = row - start
            upper = (inside >= depth).astype(jnp.int32)
            slot = owner * depth + inside - upper * depth
            here = jnp.logical_and(inside >= 0, inside < size)
            places = lax.broadcasted_iota(jnp.int32, (tok, n_sp * depth), 1)
            for side in (0, 1):
                target = jnp.where(jnp.logical_and(here, upper == side), slot, -1)
                onehot[side] = jnp.where(places == target, 1.0, 0.0).astype(BF16)

    others = pl.ds(0, (n_sp - 1) * tok)

    def wait_kind(c):
        all_arrived(
            kland.at[:, others] if c == 1 else vaug.at[:, others, pl.ds(0, hd)], r_sem.at[c]
        )
        own_copy(c).wait()

    quarter = seq // 4
    tail_ok = 3 * quarter + lax.broadcasted_iota(jnp.int32, (quarter, hd), 0) < count
    wait_kind(1)
    for h in (0, 1):
        for part in range(4):
            rows = slice(part * quarter, (part + 1) * quarter)
            block = kland[h, rows].astype(F32)
            if part == 3:
                block = jnp.where(tail_ok, block, kland[h, 0:16].astype(F32)[0:1])
            kt[h, :, rows] = block.T.astype(BF16)
    wait_kind(2)
    for h in (0, 1):
        tail = vaug[h, 3 * quarter:, :hd].astype(F32)
        vaug[h, 3 * quarter:, :hd] = jnp.where(tail_ok, tail, 0.0).astype(BF16)

    def sibling_copy(source):
        return pltpu.make_async_remote_copy(
            src_ref=att_send.at[source],
            dst_ref=att_recv.at[source],
            send_sem=sib_s,
            recv_sem=sib_r.at[source],
            device_id={"cfg": 1 - core},
            device_id_type=MESH,
        )

    def branch_copy(part, target):
        rows = pl.ds(*parts[part])
        return pltpu.make_async_remote_copy(
            src_ref=brs.at[target, rows],
            dst_ref=brl.at[me, rows],
            send_sem=br_s.at[part],
            recv_sem=br_r.at[part],
            device_id={"sp": target},
            device_id_type=MESH,
        )

    def branches(blocks, part):
        return blocks.at[pl.ds(0, n_sp - 1), pl.ds(*parts[part])]

    def attend(step):
        source = query_peer(step)
        for h in (0, 1):
            sc[h] = jnp.dot(qland[source, h], kt[h], preferred_element_type=F32)
        done = []
        for h in (0, 1):
            top = jnp.max(sc[h], axis=1, keepdims=True) * scale
            weights = jnp.exp2(sc[h] * scale - top).astype(BF16)
            mixed = jnp.dot(weights, vaug[h], preferred_element_type=F32)
            done.append(mixed[:, :hd] / mixed[:, hd:])
        att_mine[source] = jnp.where(core == 0, done[0], done[1]).astype(BF16)
        att_send[source] = jnp.where(core == 0, done[1], done[0]).astype(BF16)
        sibling_copy(source).start()

    def combine(step):
        source = query_peer(step)
        sibling_copy(source).wait_recv()
        mine = att_mine[source].astype(F32)
        theirs = att_recv[source].astype(F32)
        cond = jnp.where(core == 0, mine, theirs)
        uncond = jnp.where(core == 0, theirs, mine)
        guided = uncond + 5.0 * (cond - uncond)
        position = source * tok + lax.broadcasted_iota(jnp.int32, (tok, hd), 0)
        return source, jnp.where(position < count, gate[0:1] * guided, 0.0).astype(BF16)

    def keep(step):
        target, block = combine(step)
        brs[target] = block

    def send_part(part, step):
        branch_copy(part, query_peer(step)).start()

    own_copy(0).wait()
    attend(0)

    def first(step, carry):
        query_arrival(query_peer(step)).wait_recv()
        attend(step)

        @pl.when(step == 1)
        def _():
            source, block = combine(0)
            brl[source] = block

        @pl.when(step > 1)
        def _():
            keep(step - 1)

        return carry

    def release(step, carry):
        send_part(0, step)
        return carry

    def later(step, carry):
        query_arrival(query_peer(step)).wait_recv()
        attend(step)
        keep(step - 1)
        send_part(0, step - 1)
        return carry

    hold = n_sp - 1 if n_sp < HOLD else HOLD
    lax.fori_loop(1, hold, first, 0)
    lax.fori_loop(1, hold - 1, release, 0)
    lax.fori_loop(hold, n_sp, later, 0)
    keep(n_sp - 1)
    send_part(0, n_sp - 1)

    for part in range(1, len(parts)):
        def send_rest(step, carry, part=part):
            send_part(part, n_sp - step if part == len(parts) - 1 else step)
            return carry

        lax.fori_loop(1, n_sp, send_rest, 0)

    def swap_copy(part):
        rows = pl.ds(parts[part][0] // 2, parts[part][1] // 2)
        return pltpu.make_async_remote_copy(
            src_ref=psum_send.at[rows], dst_ref=psum_recv.at[rows],
            send_sem=ps_s.at[part], recv_sem=ps_r.at[part],
            device_id={"cfg": 1 - core}, device_id_type=MESH,
        )

    def latent_copy(part, target):
        rows = pl.ds(parts[part][0] // 2, parts[part][1] // 2)
        return pltpu.make_async_remote_copy(
            src_ref=lat_mine.at[rows], dst_ref=tables[part].at[me],
            send_sem=lat_s.at[part], recv_sem=lat_r.at[part],
            device_id={"section": 1, "sp": target}, device_id_type=MESH,
        )

    for c in (0, 1, 2):
        all_sent(stage.at[c, pl.ds(0, 2 * (n_sp - 1))], s_sem.at[c])
    all_sent(att_send, sib_s)

    wanted_copy = pltpu.make_async_copy(wanted_held, wanted_out, out_sem.at[1])
    brl_copy = pltpu.make_async_copy(brl, brl_out, out_sem.at[2])

    @pl.when(sec == 0)
    def _():
        for part, (start, size) in enumerate(parts):
            all_arrived(branches(brl, part), br_r.at[part])
            total = jnp.zeros((size, width), F32)
            for source in range(n_sp):
                total = total + lax.dot_general(
                    brl[source, start:start + size], wo[2 * source + core],
                    (((1,), (1,)), ((), ())), preferred_element_type=F32,
                )
            packed = jnp.concatenate([total[:size // 2], total[size // 2:]], axis=1)
            rows = slice(start // 2, (start + size) // 2)
            psum_send[rows] = packed
            swap_copy(part).start()
            swap_copy(part).wait_recv()
            lat_mine[rows] = (packed + psum_recv[rows]).astype(BF16)

            def hand(step, carry, part=part):
                latent_copy(part, to_peer(n_sp - 1 - step)).start()
                return carry

            lax.fori_loop(0, n_sp, hand, 0)

        wanted_held[...] = jnp.zeros_like(wanted_held)
        wanted_copy.start()
        brl_copy.start()
        for part in range(len(parts)):
            all_sent(branches(brs, part), br_s.at[part])
            all_sent(tables[part], lat_s.at[part])
            swap_copy(part).wait_send()

    @pl.when(sec == 1)
    def _():
        lanes = lax.broadcasted_iota(jnp.int32, (tok, 2 * width), 1)

        for part in range(len(parts)):
            all_arrived(branches(brl, part), br_r.at[part])
        brl_copy.start()
        for part in range(len(parts)):
            all_sent(branches(brs, part), br_s.at[part])
        picked = jnp.zeros((tok, 2 * width), F32)
        for part, (onehot, table) in enumerate(zip(onehots, tables)):
            all_arrived(table, lat_r.at[part])
            rows = table[...].reshape(n_sp * parts[part][1] // 2, 2 * width)
            low = jnp.dot(onehot[0], rows, preferred_element_type=F32)
            high = jnp.dot(onehot[1], rows, preferred_element_type=F32)
            picked = picked + jnp.where(lanes < width, low, high)
        wanted_held[...] = picked.astype(BF16)
        wanted_copy.start()

    w2_copy.wait()
    brl_copy.wait()
    wanted_copy.wait()

    @pl.when(sec == 1)
    def _():
        for c in RELAYED:
            onward(c).wait_send()


def lift_kernel(wanted_ref, w2_ref, brl_ref, out_ref):
    groups, _, hd = brl_ref.shape
    raised = jnp.dot(wanted_ref[...], w2_ref[...], preferred_element_type=F32)
    result = jnp.stack(
        [
            (brl_ref[g].astype(F32) + raised[:, g * hd:(g + 1) * hd]).astype(BF16)
            for g in range(groups)
        ]
    )
    out_ref[...] = jnp.swapaxes(result, 0, 1)


def on_device(qkv, counts, timesteps, block_map, w_out, w_in):
    n_sp = lax.axis_size("sp")
    tok, _, heads, hd = qkv.shape[2:]
    width = w_out.shape[2]
    seq = tok * n_sp
    half = tok // 2
    halves = [size // 2 for _, size in part_rows(tok)]
    dma = pltpu.SemaphoreType.DMA
    hbm = pl.BlockSpec(memory_space=pltpu.HBM)

    def body(*refs):
        kernel(n_sp, tok, heads, hd, width, *refs)

    brl, wanted, w2 = pl.pallas_call(
        body,
        name="guided_attention",
        out_shape=(
            jax.ShapeDtypeStruct((n_sp, tok, hd), BF16),
            jax.ShapeDtypeStruct((tok, 2 * width), BF16),
            jax.ShapeDtypeStruct((2 * width, heads // 2 * hd), BF16),
        ),
        in_specs=[hbm] * 6,
        out_specs=(hbm, hbm, hbm),
        scratch_shapes=[
            pltpu.VMEM((3, tok, heads, hd), BF16),
            pltpu.VMEM((3, heads, tok, hd), BF16),
            pltpu.VMEM((n_sp, 2, tok, hd), BF16),
            pltpu.VMEM((2, seq, hd), BF16),
            pltpu.VMEM((2, seq, 2 * hd), BF16),
            pltpu.VMEM((2, hd, seq), BF16),
            pltpu.VMEM((2, tok, seq), F32),
            pltpu.VMEM((n_sp, tok, hd), BF16),
            pltpu.VMEM((n_sp, tok, hd), BF16),
            pltpu.VMEM((n_sp, tok, hd), BF16),
            pltpu.VMEM((n_sp, tok, hd), BF16),
            pltpu.VMEM((n_sp, tok, hd), BF16),
            pltpu.VMEM((2, 2, tok, hd), BF16),
            pltpu.VMEM((half, 2 * width), BF16),
            *[pltpu.VMEM((n_sp, depth, 2 * width), BF16) for depth in halves],
            pltpu.VMEM((half, 2 * width), F32),
            pltpu.VMEM((half, 2 * width), F32),
            *[pltpu.VMEM((2, tok, n_sp * depth), BF16) for depth in halves],
            pltpu.VMEM((heads, width, hd), BF16),
            pltpu.VMEM((width, heads, hd), BF16),
            pltpu.VMEM((8, hd), F32),
            pltpu.VMEM((tok, 2 * width), BF16),
            pltpu.VMEM((2 * width, heads // 2 * hd), BF16),
            pltpu.SMEM((1, 1), jnp.int32),
            pltpu.SMEM((1, 1), jnp.int32),
            pltpu.VMEM((1, tok), jnp.int32),
            dma((3,)), dma((5,)), dma((3,)),
            dma((3,)), dma((3,)), dma((n_sp,)),
            dma, dma((n_sp,)),
            dma((3,)), dma((3,)),
            dma((3,)), dma((3,)),
            dma((3,)), dma((3,)),
            dma((2,)), dma((2,)), dma((3,)),
        ],
        compiler_params=pltpu.CompilerParams(
            collective_id=0, has_side_effects=True, vmem_limit_bytes=56 << 20
        ),
    )(
        qkv[0, 0],
        counts,
        timesteps,
        block_map.reshape(1, tok),
        jnp.swapaxes(w_out, 1, 2),
        w_in,
    )
    result = pl.pallas_call(
        lift_kernel,
        name="lift",
        out_shape=jax.ShapeDtypeStruct((tok, heads // 2, hd), BF16),
    )(wanted, w2, brl)
    return result[None, :, None]


def solution(mesh):
    placed = (
        P("section", "cfg", ("req", "sp"), None, None, None),
        P("section", "req"),
        P("section", "req"),
        P(("req", "sp")),
        P(),
        P(),
    )
    return jax.shard_map(
        on_device,
        mesh=mesh,
        in_specs=placed,
        out_specs=P("section", ("req", "sp"), "cfg", None, None),
        check_vma=False,
    )
```
